32 devices in a mesh: shard: 4 (over z), heads: 2 (over core), tensor: 4 (over y, x).
Axes of the slice: x: 2, y: 2, z: 4, core: 2. Of those that a mesh axis runs over, the one named last changes fastest.
Arguments:
- block_input: bfloat16 [2048, 1024], P('shard'), may hold values from -6 to 6
- attn_gain: bfloat16 [1024], P('shard'), may hold values from 0.25 to 1.75
- query_weight: bfloat16 [1024, 1024], P('shard', 'heads'), may hold values from -0.1875 to 0.1875
- key_weight: bfloat16 [1024, 512], P('shard', 'heads'), may hold values from -0.1875 to 0.1875
- value_weight: bfloat16 [1024, 512], P('shard', 'heads'), may hold values from -0.1875 to 0.1875
- query_gain: bfloat16 [64], replicated, may hold values from 0.25 to 1.75
- key_gain: bfloat16 [64], replicated, may hold values from 0.25 to 1.75
- output_weight: bfloat16 [1024, 1024], P('heads', 'shard'), may hold values from -1.5 to 1.5
- ffn_gain: bfloat16 [1024], P('shard'), may hold values from 0.25 to 1.75
- gate_weight: bfloat16 [1024, 4608], P('shard', 'tensor'), may hold values from -0.1875 to 0.1875
- up_weight: bfloat16 [1024, 4608], P('shard', 'tensor'), may hold values from -0.1875 to 0.1875
- down_weight: bfloat16 [4608, 1024], P('tensor', 'shard'), may hold values from -0.09375 to 0.09375
- lengths: int32 [16], replicated, may hold values from 8 to 1792, as said below
- packing: int32 [16], replicated, may hold values from 0 to 15, each once
- out_grad: bfloat16 [2048, 1024], P('shard'), may hold values from -6 to 6
Outputs:
- block_output: bfloat16 [2048, 1024], P('shard')
- input_grad: float32 [2048, 1024], P('shard')
- attn_gain_grad: float32 [1024], P('shard')
- query_weight_grad: float32 [1024, 1024], P('shard', 'heads')
- key_weight_grad: float32 [1024, 512], P('shard', 'heads')
- value_weight_grad: float32 [1024, 512], P('shard', 'heads')
- query_gain_grad: float32 [64], replicated
- key_gain_grad: float32 [64], replicated
- output_weight_grad: float32 [1024, 1024], P('heads', 'shard')
- ffn_gain_grad: float32 [1024], P('shard')
- gate_weight_grad: float32 [1024, 4608], P('shard', 'tensor')
- up_weight_grad: float32 [1024, 4608], P('shard', 'tensor')
- down_weight_grad: float32 [4608, 1024], P('tensor', 'shard')
The draws below stay inside these ranges and needn't reach their ends.
Inputs may be any that keep to these rules, and one draw needn't show every extreme that they name: `lengths`: one sequence, at an index drawn from the seed, has exactly 1792 tokens; the other 15 have 8 to 16, one of them exactly 8; they are packed from slot 0 in the order of packing, and the slots after them are padding.
All inputs are finite; a program needn't handle non-finite values.
Results may differ from the reference program's by a relative error of at most 0.018.
Values may be sent and summed in bfloat16 or wider, within the bound.
No kernel may reach another device: no remote copies, remote signals or barrier semaphores. Data moves between devices by JAX's collectives and lax.ppermute only.
A program may use at most 128 MiB of HBM per device.

```python
import math
import jax
import jax.numpy as jnp
from jax import lax

D = 1024
HQ = 16
KV = 8
HD = 64
FF = 4608
NSEQ = 16
TOKENS = 2048
LONG_LEN = 1792
SHORT_MIN = 8
SHORT_MAX = 16


def draw_lengths(key, part):
    key = jax.random.fold_in(key, 11)
    order_key, size_key = jax.random.split(key)
    order = jax.random.permutation(order_key, NSEQ)
    shorts = jax.random.randint(size_key, (NSEQ,), SHORT_MIN, SHORT_MAX + 1)
    places = jnp.arange(NSEQ)
    lengths = jnp.where(places == order[0], LONG_LEN, jnp.where(places == order[1], SHORT_MIN, shorts))
    return lengths.astype(jnp.int32)


def levels(stream_key, extent, cuts, low, largest):
    gain, own = 1.0, jax.random.fold_in(stream_key, 6)
    for axis_at, shards_of in cuts:
        steps = jnp.exp(jax.random.uniform(jax.random.fold_in(own, axis_at), (shards_of,), jnp.float32, low / len(cuts), largest / len(cuts)))
        gain = gain * jnp.repeat(steps, extent[axis_at] // shards_of).reshape([-1 if axis == axis_at else 1 for axis in range(len(extent))])
    return gain


def scatter_about(own_key, dims, scale, limit, cuts=(), kind=jnp.bfloat16):
    drawn = scale * jax.random.normal(own_key, dims, jnp.float32)
    if cuts:
        drawn = drawn * levels(own_key, dims, cuts, -0.22, 0.18)
    return jnp.clip(drawn, -limit, limit).astype(kind)


def setup_inputs(seed: int = 0) -> dict:
    key_list = jax.random.split(jax.random.key(seed), 16)
    return {
        "block_input": scatter_about(key_list[0], (TOKENS, D), 1.0, 6.0, ((0, 4),)),
        "attn_gain": jnp.clip(1.0 + 0.15 * jax.random.normal(key_list[1], (D,), jnp.float32), 0.25, 1.75).astype(jnp.bfloat16),
        "query_weight": scatter_about(key_list[2], (D, HQ * HD), D ** -0.5, 0.1875, ((0, 4), (1, 2))),
        "key_weight": scatter_about(key_list[3], (D, KV * HD), D ** -0.5, 0.1875, ((0, 4), (1, 2))),
        "value_weight": scatter_about(key_list[4], (D, KV * HD), D ** -0.5, 0.1875, ((0, 4), (1, 2))),
        "query_gain": jnp.clip(1.0 + 0.15 * jax.random.normal(key_list[5], (HD,), jnp.float32), 0.25, 1.75).astype(jnp.bfloat16),
        "key_gain": jnp.clip(1.0 + 0.15 * jax.random.normal(key_list[6], (HD,), jnp.float32), 0.25, 1.75).astype(jnp.bfloat16),
        "output_weight": scatter_about(key_list[7], (HQ * HD, D), (max(1, HQ * HD // 64)) ** -0.5, 1.5, ((0, 2), (1, 4))),
        "ffn_gain": jnp.clip(1.0 + 0.15 * jax.random.normal(key_list[8], (D,), jnp.float32), 0.25, 1.75).astype(jnp.bfloat16),
        "gate_weight": scatter_about(key_list[9], (D, FF), D ** -0.5, 0.1875, ((0, 4), (1, 4))),
        "up_weight": scatter_about(key_list[10], (D, FF), D ** -0.5, 0.1875, ((0, 4), (1, 4))),
        "down_weight": scatter_about(key_list[11], (FF, D), FF ** -0.5, 0.09375, ((0, 4), (1, 4))),
        "lengths": draw_lengths(jax.random.fold_in(key_list[15], 71), 0),
        "packing": jax.random.permutation(key_list[13], NSEQ).astype(jnp.int32),
        "out_grad": scatter_about(key_list[14], (TOKENS, D), 1.0, 6.0, ((0, 4),)),
    }


EPSILON = 1e-05
ROPE_THETA = 1000000.0
MASKED_SCORE = -1e+30

@jax.custom_vjp
def low(v):
    return lax.optimization_barrier(v.astype(jnp.bfloat16)).astype(jnp.float32)

@jax.custom_vjp
def low_back(v):
    return v

def low_keep(v):
    return (low(v), None)

def low_pass(kept, grad):
    return (grad,)

def back_keep(v):
    return (v, None)

def back_low(kept, grad):
    return (low(grad),)
low.defvjp(low_keep, low_pass)
low_back.defvjp(back_keep, back_low)

def exact_dot(left_side, right_side):
    return jnp.dot(left_side, right_side, precision=lax.Precision.HIGHEST, preferred_element_type=jnp.float32)

def scale_rows(values, gain_vector):
    return values * lax.rsqrt(lax.optimization_barrier(jnp.mean(values * values, axis=-1, keepdims=True)) + EPSILON) * gain_vector

def layout(lengths, packing, first_row, row_count):
    sequence_count = lengths.shape[0]
    chosen = (packing[:, None] == jnp.arange(sequence_count, dtype=jnp.int32)[None, :]).astype(jnp.int32)
    packed = lax.optimization_barrier(jnp.sum(chosen * lengths[None, :], axis=1)).astype(jnp.int32)
    seq_ends = jnp.cumsum(packed).astype(jnp.int32)
    token_index = (first_row + jnp.arange(row_count, dtype=jnp.int32)).astype(jnp.int32)
    passed = token_index[:, None] >= seq_ends[None, :]
    segment = lax.optimization_barrier(jnp.sum(passed.astype(jnp.int32), axis=1)).astype(jnp.int32)
    seq_start = lax.optimization_barrier(jnp.sum(jnp.where(passed, packed[None, :], 0), axis=1)).astype(jnp.int32)
    position = (token_index - seq_start).astype(jnp.float32)
    live_rows = segment < sequence_count
    return (token_index, segment, position, live_rows)

def rotary_tables(position, width):
    half_width = width // 2
    exponents = jnp.arange(half_width, dtype=jnp.float32) * (2.0 / width)
    frequency = jnp.power(jnp.float32(ROPE_THETA), -exponents)
    angles = position[:, None] * frequency[None, :]
    cosine_table = jnp.concatenate([jnp.cos(angles), jnp.cos(angles)], axis=-1)[:, None, :]
    sine_table = jnp.concatenate([jnp.sin(angles), jnp.sin(angles)], axis=-1)[:, None, :]
    return (cosine_table, sine_table)

def rotate(values, cosine_table, sine_table):
    half_width = values.shape[-1] // 2
    turned = jnp.concatenate([-values[..., half_width:], values[..., :half_width]], axis=-1)
    return values * cosine_table + turned * sine_table

def allowed_keys(block_start, block_rows, query_index, query_segment, query_live, key_index, key_segment):
    query_rows = lax.dynamic_slice_in_dim(query_index, block_start, block_rows)
    query_segs = lax.dynamic_slice_in_dim(query_segment, block_start, block_rows)
    query_alive = lax.dynamic_slice_in_dim(query_live, block_start, block_rows)
    same_seq = query_segs[:, None] == key_segment[None, :]
    causal = key_index[None, :] <= query_rows[:, None]
    itself = key_index[None, :] == query_rows[:, None]
    return same_seq & causal & (query_alive[:, None] | itself)

def attend(query_rot, key_rot, value_heads, token_index, segment, live_rows):
    row_count = query_rot.shape[0]
    block_rows = math.gcd(row_count, 512)
    group_size = HQ // KV
    score_scale = 1.0 / math.sqrt(HD)

    def one_block(block_start):
        queries = lax.dynamic_slice_in_dim(query_rot, block_start, block_rows, 0).reshape(block_rows, KV, group_size, HD)
        allowed = allowed_keys(block_start, block_rows, token_index, segment, live_rows, token_index, segment)
        score = low_back(jnp.einsum('qgrd,kgd->grqk', queries, key_rot, precision=lax.Precision.HIGHEST) * score_scale)
        score = jnp.where(allowed[None, None], score, MASKED_SCORE)
        unscaled = jnp.exp(score - lax.optimization_barrier(jnp.max(score, axis=-1, keepdims=True)))
        probabilities = low(unscaled / lax.optimization_barrier(jnp.sum(unscaled, axis=-1, keepdims=True)))
        block_out = jnp.einsum('grqk,kgd->qgrd', probabilities, value_heads, precision=lax.Precision.HIGHEST)
        return block_out.reshape(block_rows, HQ * HD)
    block_starts = (jnp.arange(row_count // block_rows, dtype=jnp.int32) * block_rows).astype(jnp.int32)
    return lax.map(jax.checkpoint(one_block), block_starts).reshape(row_count, HQ * HD)

def forward(inputs, attn_gain, query_weight, key_weight, value_weight, query_gain, key_gain, output_weight, ffn_gain, gate_weight, up_weight, down_weight, token_index, segment, position, live_rows):
    row_count = inputs.shape[0]
    normed_one = low(scale_rows(inputs, attn_gain))
    query_heads = low_back(exact_dot(normed_one, query_weight)).reshape(row_count, HQ, HD)
    key_heads = low_back(exact_dot(normed_one, key_weight)).reshape(row_count, KV, HD)
    value_heads = low(low_back(exact_dot(normed_one, value_weight))).reshape(row_count, KV, HD)
    cosine_table, sine_table = rotary_tables(position, HD)
    query_rot = low(rotate(scale_rows(query_heads, query_gain), cosine_table, sine_table))
    key_rot = low(rotate(scale_rows(key_heads, key_gain), cosine_table, sine_table))
    attended = low(low_back(attend(query_rot, key_rot, value_heads, token_index, segment, live_rows)))
    middle = inputs + low_back(exact_dot(attended, output_weight))
    normed_two = low(scale_rows(middle, ffn_gain))
    gate_value = low_back(exact_dot(normed_two, gate_weight))
    up_value = low_back(exact_dot(normed_two, up_weight))
    hidden = low(jax.nn.silu(gate_value) * up_value)
    result = middle + low_back(exact_dot(hidden, down_weight))
    return result * live_rows.astype(jnp.float32)[:, None]

def reference(block_input, attn_gain, query_weight, key_weight, value_weight, query_gain, key_gain, output_weight, ffn_gain, gate_weight, up_weight, down_weight, lengths, packing, out_grad):
    row_count = block_input.shape[0]
    token_index, segment, position, live_rows = layout(lengths, packing, 0, row_count)
    floats = [argument.astype(jnp.float32) for argument in (block_input, attn_gain, query_weight, key_weight, value_weight, query_gain, key_gain, output_weight, ffn_gain, gate_weight, up_weight, down_weight)]

    def whole_block(*params):
        return forward(*params, token_index, segment, position, live_rows)
    result, pullback = jax.vjp(whole_block, *floats)
    gradients = pullback(out_grad.astype(jnp.float32))
    return (result.astype(jnp.bfloat16), gradients[0], gradients[1], gradients[2], gradients[3], gradients[4], gradients[5], gradients[6], gradients[7], gradients[8], gradients[9], gradients[10], gradients[11])
```

```python
import math

import jax
import jax.numpy as jnp
from jax import lax
from jax.experimental import pallas as pl
from jax.experimental.pallas import tpu as pltpu
from jax.sharding import PartitionSpec as P

EPSILON = 1e-05
ROPE_THETA = 1000000.0
BF = jnp.bfloat16
F32 = jnp.float32
MIB = 1 << 20
GAIN_ROWS = 16


def nn_dot(a, b):
    return lax.dot_general(a, b, (((1,), (0,)), ((), ())), preferred_element_type=F32)


def nt_dot(a, b):
    return lax.dot_general(a, b, (((1,), (1,)), ((), ())), preferred_element_type=F32)


def tn_dot(a, b):
    return lax.dot_general(a, b, (((0,), (0,)), ((), ())), preferred_element_type=F32)


def call(kernel, outs, ids, arrays, scratch=(), vmem=32, flops=0, name=None):
    shapes = [jax.ShapeDtypeStruct(s, d) for s, d in outs]
    moved = sum(a.size * a.dtype.itemsize for a in arrays)
    moved += sum(math.prod(s.shape) * s.dtype.itemsize for s in shapes)
    return pl.pallas_call(
        kernel,
        out_shape=shapes,
        in_specs=[pl.BlockSpec(memory_space=pltpu.SMEM)]
        + [pl.BlockSpec(memory_space=pltpu.VMEM) for _ in arrays],
        out_specs=[pl.BlockSpec(memory_space=pltpu.VMEM) for _ in shapes],
        scratch_shapes=list(scratch),
        compiler_params=pltpu.CompilerParams(vmem_limit_bytes=vmem * MIB),
        cost_estimate=pl.CostEstimate(flops=int(flops), bytes_accessed=int(moved), transcendentals=0),
        name=name,
    )(ids, *arrays)


def lanes(shape):
    return lax.broadcasted_iota(jnp.int32, shape, 1)


def head_mean(v, low):
    first = jnp.sum(jnp.where(low, v, 0.0), axis=1, keepdims=True)
    second = jnp.sum(jnp.where(low, 0.0, v), axis=1, keepdims=True)
    return jnp.where(low, first, second) * (1.0 / 64.0)


def turn(v, first):
    return jnp.where(first, -pltpu.roll(v, 96, 1), pltpu.roll(v, 32, 1))


def turn_back(v, first):
    return jnp.where(first, pltpu.roll(v, 96, 1), -pltpu.roll(v, 32, 1))


def make(mesh):
    n_shard, n_heads, n_tensor = (mesh.shape[a] for a in ("shard", "heads", "tensor"))
    blocks_mode = n_shard == 4
    n_plane = n_heads * n_tensor

    def swap(x, axis, k):
        size = mesh.shape[axis]
        return lax.ppermute(x, axis, [(i, i ^ k) for i in range(size)])

    def shard_blocks(x, staged):
        one, two = swap(x, "shard", 1), swap(x, "shard", 2)
        three = swap(two, "shard", 1) if staged else swap(x, "shard", 3)
        return [x, one, two, three]

    def plane_blocks(x):
        same = [x] + [swap(x, "tensor", k) for k in range(1, n_tensor)]
        found = list(same)
        for i in range(1, n_heads):
            found += [swap(s, "heads", i) for s in same]
        return found

    def plane_index(ids, b):
        return (ids[1] ^ (b // n_tensor)) * n_tensor + (ids[2] ^ (b % n_tensor))

    def on_device(
        block_input,
        attn_gain,
        query_weight,
        key_weight,
        value_weight,
        query_gain,
        key_gain,
        output_weight,
        ffn_gain,
        gate_weight,
        up_weight,
        down_weight,
        lengths,
        packing,
        out_grad,
    ):
        rows, width = block_input.shape
        depth = query_weight.shape[0]
        head = query_gain.shape[0]
        hidden_all = gate_weight.shape[1]
        hid = hidden_all // n_heads
        q_cols = query_weight.shape[1] // n_tensor
        k_cols = key_weight.shape[1] // n_tensor
        n_block = n_shard if blocks_mode else 1
        wide = width // n_block
        sub = rows // n_plane
        half = rows // n_heads
        z, h, t = (lax.axis_index(a) for a in ("shard", "heads", "tensor"))
        ids = jnp.stack([z, h, t]).astype(jnp.int32)

        def owner(ids_ref, k):
            return ids_ref[0] ^ k

        def offset(ids_ref, k):
            return pl.multiple_of(owner(ids_ref, k) * wide, wide) if blocks_mode else 0

        count = lengths.shape[0]
        order = jnp.arange(count, dtype=jnp.int32)
        packed = jnp.sum(jnp.where(packing[:, None] == order[None, :], lengths[None, :], 0), axis=1)
        ends = jnp.sum(jnp.where(order[None, :] <= order[:, None], packed[None, :], 0), axis=1)
        token = z * rows + jnp.arange(rows, dtype=jnp.int32)
        passed = token[:, None] >= ends[None, :]
        segment = jnp.sum(passed.astype(jnp.int32), axis=1)
        start = jnp.sum(jnp.where(passed, packed[None, :], 0), axis=1)
        live = segment < count
        lowest = jnp.where(live, start, token)
        row_info = jnp.where(
            lax.broadcasted_iota(jnp.int32, (rows, 128), 1) == 0,
            lowest[:, None].astype(F32),
            live[:, None].astype(F32),
        )
        exponents = jnp.arange(head // 2, dtype=F32) * (2.0 / head)
        frequency = jnp.power(jnp.float32(ROPE_THETA), -exponents)
        angles = (token - start).astype(F32)[:, None] * jnp.tile(frequency, 4)[None, :]
        cosine, sine = jnp.cos(angles), jnp.sin(angles)
        head_gains = jnp.broadcast_to(
            jnp.stack(
                [
                    jnp.tile(query_gain.astype(F32), 2),
                    jnp.concatenate([key_gain.astype(F32), jnp.ones((head,), F32)]),
                ]
            )[:, None, :],
            (2, 8, 128),
        ).reshape(16, 128)

        own_qkv = jnp.concatenate(
            [
                lax.dynamic_slice_in_dim(query_weight, t * q_cols, q_cols, 1),
                lax.dynamic_slice_in_dim(key_weight, t * k_cols, k_cols, 1),
                lax.dynamic_slice_in_dim(value_weight, t * k_cols, k_cols, 1),
            ],
            axis=1,
        )
        own_out = lax.dynamic_slice_in_dim(output_weight, t * q_cols, q_cols, 0)
        first_core = h == 0
        own_gate_up = jnp.where(
            first_core,
            jnp.concatenate([gate_weight[:, :hid], up_weight[:, :hid]], axis=1),
            jnp.concatenate([gate_weight[:, hid:], up_weight[:, hid:]], axis=1),
        )
        own_down = lax.dynamic_slice_in_dim(down_weight, h * hid, hid, 0)
        gains = jnp.concatenate(
            [attn_gain[None], ffn_gain[None], jnp.zeros((GAIN_ROWS - 2, depth), BF)], axis=0
        )
        if blocks_mode:
            qkv_parts = shard_blocks(jnp.concatenate([own_qkv, gains], axis=0), False)
            gain_parts = []
            out_parts = shard_blocks(own_out, False)
            gate_up_parts = shard_blocks(own_gate_up, True)
            down_parts = shard_blocks(own_down, True)
        else:
            gather = lambda x, axis: [lax.all_gather(x, "shard", axis=axis, tiled=True)]
            qkv_parts = gather(own_qkv, 0)
            gain_parts = gather(gains, 1)
            out_parts = gather(own_out, 1)
            gate_up_parts = gather(own_gate_up, 0)
            down_parts = gather(own_down, 1)

        def project(ids_ref, x_ref, cos_ref, sin_ref, hg_ref, *refs):
            w_refs, refs = refs[:n_block], refs[n_block:]
            g_refs, refs = refs[: len(gain_parts)], refs[len(gain_parts) :]
            n_ref, raw_ref, qs_ref, kv_ref, ga_ref, gf_ref = refs
            for k in range(n_block):
                both = (g_refs[0][...] if g_refs else w_refs[k][wide:, :]).astype(F32)
                where = pl.ds(offset(ids_ref, k), wide)
                ga_ref[:, where] = jnp.broadcast_to(both[0:1], (8, wide))
                gf_ref[:, where] = jnp.broadcast_to(both[1:2], (8, wide))
            step = 128

            def body(c, carry):
                at = pl.ds(pl.multiple_of(c * step, step), step)
                x = x_ref[at, :].astype(F32)
                r = lax.rsqrt(jnp.mean(x * x, axis=1, keepdims=True) + EPSILON)
                n_ref[at, :] = (x * r * ga_ref[0:1, :]).astype(BF)
                acc = jnp.zeros((step, 256), F32)
                for k in range(n_block):
                    acc += nn_dot(n_ref[at, pl.ds(offset(ids_ref, k), wide)], w_refs[k][:wide, :])
                raw_ref[at, :] = acc
                lane = lanes((step, 128))
                low, first = lane < 64, (lane % 64) < 32
                cos, sin = cos_ref[at, :], sin_ref[at, :]
                q, kv = acc[:, :128], acc[:, 128:]
                q = q * lax.rsqrt(head_mean(q * q, low) + EPSILON) * hg_ref[0:1, :]
                q = (q * cos + turn(q, first) * sin).astype(BF).astype(F32) * (1.0 / math.sqrt(head))
                qs_ref[at, :] = jnp.where(low, q, 0.0).astype(BF)
                qs_ref[pl.ds(pl.multiple_of(rows + c * step, step), step), :] = jnp.where(
                    low, pltpu.roll(q, 64, 1), 0.0
                ).astype(BF)
                k_ = kv * lax.rsqrt(head_mean(kv * kv, low) + EPSILON) * hg_ref[8:9, :]
                k_ = k_ * cos + turn(k_, first) * sin
                kv_ref[at, :] = jnp.where(low, k_, kv).astype(BF)
                return carry

            lax.fori_loop(0, rows // step, body, 0)

        normed_one, raw, queries, own_kv, ga, gf = call(
            project,
            [
                ((rows, width), BF),
                ((rows, 256), F32),
                ((2 * rows, 128), BF),
                ((rows, 128), BF),
                ((8, width), F32),
                ((8, width), F32),
            ],
            ids,
            [block_input, cosine, sine, head_gains, *qkv_parts, *gain_parts],
            flops=2 * rows * width * 256,
            vmem=24,
            name="project",
        )
        if blocks_mode:
            kv_parts = shard_blocks(own_kv, False)
        else:
            kv_parts = [lax.all_gather(own_kv, "shard", axis=0, tiled=True)]

        chunk = 256

        def over_keys(ids_ref, kv_refs, block):
            if blocks_mode:
                for k in range(n_block):
                    pl.when(owner(ids_ref, k) <= ids_ref[0])(
                        lambda k=k: block(owner(ids_ref, k), kv_refs[k], 0)
                    )
            else:

                def step(j, carry):
                    block(j, kv_refs[0], pl.multiple_of(j * rows, rows))
                    return carry

                lax.fori_loop(0, ids_ref[0] + 1, step, 0)

        def masked_exp(ids_ref, info_ref, score, c, own):
            row = (c * chunk) % rows
            at = pl.ds(pl.multiple_of(row, chunk), chunk)
            col = lanes((chunk, rows))
            lowest_ = info_ref[at, 0:1].astype(jnp.int32) - own * rows
            mine = lax.broadcasted_iota(jnp.int32, (chunk, 1), 0) + (row + (ids_ref[0] - own) * rows)
            return jnp.where((col >= lowest_) & (col <= mine), jnp.exp(score), 0.0)

        def attend(ids_ref, info_ref, qs_ref, *refs):
            kv_refs, (att_ref, oa_ref, acc_ref) = refs[:n_block], refs[n_block:]
            acc_ref[...] = jnp.zeros_like(acc_ref)
            low = lanes((rows, 128)) < 64

            def block(own, kv_ref, base):
                kv = kv_ref[pl.ds(base, rows), :]
                counted = jnp.where(low, 1.0, kv.astype(F32)).astype(BF)

                def body(c, carry):
                    at = pl.ds(pl.multiple_of(c * chunk, chunk), chunk)
                    p = masked_exp(ids_ref, info_ref, nt_dot(qs_ref[at, :], kv), c, own)
                    acc_ref[at, :] += nn_dot(p.astype(BF), counted)
                    return carry

                lax.fori_loop(0, 2 * rows // chunk, body, 0)

            over_keys(ids_ref, kv_refs, block)
            for i in range(2):
                acc = acc_ref[i * rows : (i + 1) * rows, :]
                inverse = 1.0 / jnp.where(low, acc, 1.0)
                done = jnp.where(low, inverse, acc * pltpu.roll(inverse, 64, 1))
                oa_ref[i * rows : (i + 1) * rows, :] = done
            att_ref[...] = jnp.where(
                low, pltpu.roll(oa_ref[:rows, :], 64, 1), oa_ref[rows:, :]
            ).astype(BF)

        attended, out_and_inverse = call(
            attend,
            [((rows, 128), BF), ((2 * rows, 128), F32)],
            ids,
            [row_info, queries, *kv_parts],
            scratch=[pltpu.VMEM((2 * rows, 128), F32)],
            flops=4 * 2 * rows * rows * n_shard * 128,
            vmem=32,
            name="attend",
        )
        attended_parts = plane_blocks(attended)

        if blocks_mode:

            def beside(ids_ref, *refs):
                for k in range(n_block):
                    refs[-1][:, pl.ds(offset(ids_ref, k), wide)] = refs[k][...]

            (own_rows,) = call(beside, [((q_cols, width), BF)], ids, out_parts, vmem=8, name="beside")
        else:
            own_rows = out_parts[0]
        row_parts = plane_blocks(own_rows)

        def below(ids_ref, *refs):
            for b in range(n_plane):
                at = pl.multiple_of(plane_index(ids_ref, b) * q_cols, q_cols)
                refs[-1][pl.ds(at, q_cols), :] = refs[b][...]

        (out_full,) = call(below, [((width, width), BF)], ids, row_parts, vmem=12, name="below")

        def middle_part(ids_ref, info_ref, x_ref, og_ref, gf_ref, wo_ref, *refs):
            a_refs, refs = refs[:n_plane], refs[n_plane:]
            gu_refs, refs = refs[:n_block], refs[n_block:]
            dn_refs, refs = refs[:n_block], refs[n_block:]
            send_ref, keep_ref, n2_ref, dgu_ref, hid_ref, cot_ref, mid_ref, gp_ref = refs[:8]
            a_ref, dn_ref = refs[8:]
            for b in range(n_plane):
                at = pl.multiple_of(plane_index(ids_ref, b) * q_cols, q_cols)
                a_ref[:, pl.ds(at, q_cols)] = a_refs[b][...]
            gp_ref[...] = jnp.zeros_like(gp_ref)
            step = half
            padded = -(-hid // 128) * 128
            whole = 2 * hid

            def body(c, carry):
                at = pl.ds(pl.multiple_of(c * step, step), step)
                middle = x_ref[at, :].astype(F32) + nn_dot(a_ref[at, :], wo_ref[...])
                mid_ref[at, :] = middle
                r = lax.rsqrt(jnp.mean(middle * middle, axis=1, keepdims=True) + EPSILON)
                n2_ref[at, :] = (middle * r * gf_ref[0:1, :]).astype(BF)
                cot_ref[at, :] = (og_ref[at, :].astype(F32) * info_ref[at, 1:2]).astype(BF)
                gu = jnp.zeros((step, whole), F32)
                dh = jnp.zeros((step, hid), F32)
                for k in range(n_block):
                    cols = pl.ds(offset(ids_ref, k), wide)
                    gu += nn_dot(n2_ref[at, cols], gu_refs[k][...])
                    dh += nt_dot(cot_ref[at, cols], dn_refs[k][...])
                gate = gu[:, :padded]
                up = pltpu.roll(gu, whole - hid, 1)[:, :padded]
                dh = jnp.concatenate([dh, jnp.zeros((step, padded - hid), F32)], axis=1) if padded > hid else dh
                sig = 1.0 / (1.0 + jnp.exp(-gate))
                act = gate * sig
                hid_ref[at, :] = (act * up)[:, :hid].astype(BF)
                d_gate = dh * up * sig * (1.0 + gate * (1.0 - sig))
                d_up = dh * act
                rest = jnp.zeros((step, whole - padded), F32)
                d_gate = jnp.concatenate([d_gate, rest], axis=1)
                d_up = pltpu.roll(jnp.concatenate([d_up, rest], axis=1), hid, 1)
                dgu_ref[at, :] = jnp.where(lanes((step, whole)) < hid, d_gate, d_up).astype(BF)
                for k in range(n_block):
                    dn_ref[:, pl.ds(offset(ids_ref, k), wide)] = nt_dot(dgu_ref[at, :], gu_refs[k][...])
                dn = dn_ref[...]
                gp_ref[...] += jnp.broadcast_to(
                    jnp.sum(dn * (mid_ref[at, :] * r), axis=0, keepdims=True), gp_ref.shape
                )
                low_dn = dn.astype(BF)

                @pl.when(c == ids_ref[1])
                def _():
                    keep_ref[...] = low_dn

                @pl.when(c != ids_ref[1])
                def _():
                    send_ref[...] = low_dn

                return carry

            lax.fori_loop(0, n_heads, body, 0)

        dn_send, dn_keep, normed_two, d_gate_up, hidden, cot, middle, ffn_gain_part = call(
            middle_part,
            [
                ((half, width), BF),
                ((half, width), BF),
                ((rows, width), BF),
                ((rows, 2 * hid), BF),
                ((rows, hid), BF),
                ((rows, width), BF),
                ((rows, width), F32),
                ((8, width), F32),
            ],
            ids,
            [row_info, block_input, out_grad, gf, out_full, *attended_parts, *gate_up_parts, *down_parts],
            scratch=[pltpu.VMEM((rows, width), BF), pltpu.VMEM((half, width), F32)],
            flops=2 * rows * width * (width + 5 * hid),
            vmem=48,
            name="middle",
        )

        def split(ids_ref, keep_ref, got_ref, *outs):
            for k in range(n_tensor):
                at = pl.ds(pl.multiple_of((ids_ref[2] ^ k) * sub, sub), sub)
                total = keep_ref[at, :].astype(F32) + got_ref[at, :].astype(F32)
                outs[k][...] = total.astype(BF)

        def plane_sum_parts(keep, send):
            got = swap(send, "heads", 1)
            parts = call(split, [((sub, width), BF)] * n_tensor, ids, [keep, got], vmem=8, name="split")
            return [parts[0]] + [swap(parts[k], "tensor", k) for k in range(1, n_tensor)]

        def tree(values):
            while len(values) > 1:
                values = [values[i] + values[i + 1] for i in range(0, len(values), 2)]
            return values[0]

        dn_parts = plane_sum_parts(dn_keep, dn_send)

        def ffn_grads(ids_ref, n2_ref, dgu_ref, hid_ref, cot_ref, *refs):
            dn_refs, (ggu_ref, gdn_ref, fo_ref) = refs[:n_block], refs[n_block:]
            for k in range(n_block):
                cols = pl.ds(offset(ids_ref, k), wide)
                ggu_ref[cols, :] = tn_dot(n2_ref[:, cols], dgu_ref[...]).astype(BF)
                down = tn_dot(hid_ref[...], cot_ref[:, cols]).astype(BF)
                if blocks_mode:
                    gdn_ref[pl.ds(pl.multiple_of(owner(ids_ref, k) * hid, hid), hid), :] = down
                else:
                    gdn_ref[...] = down
                fo_ref[:, cols] = nn_dot(hid_ref[...], dn_refs[k][...]).astype(BF)

        grad_gate_up, grad_down, ffn_part = call(
            ffn_grads,
            [((width, 2 * hid), BF), ((n_block * hid, wide), BF), ((rows, width), BF)],
            ids,
            [normed_two, d_gate_up, hidden, cot, *down_parts],
            flops=2 * rows * width * 4 * hid,
            vmem=32,
            name="ffn_grads",
        )
        gate_up_sum = lax.psum_scatter(grad_gate_up, "shard", scatter_dimension=0, tiled=True)
        down_sum = lax.psum_scatter(
            grad_down, "shard", scatter_dimension=0 if blocks_mode else 1, tiled=True
        )
        ffn_out = lax.psum(ffn_part, ("heads", "tensor")).astype(F32)
        live_weight = live.astype(F32)[:, None]
        block_output = (live_weight * (middle + ffn_out)).astype(BF)

        def norm_two_back(ids_ref, mid_ref, cot_ref, gf_ref, *refs):
            part_refs, (dm_ref, da_ref) = refs[:n_tensor], refs[n_tensor:]
            at = pl.ds(pl.multiple_of((ids_ref[1] * n_tensor + ids_ref[2]) * sub, sub), sub)
            d = tree([p[...].astype(F32) for p in part_refs])
            v = mid_ref[at, :]
            r = lax.rsqrt(jnp.mean(v * v, axis=1, keepdims=True) + EPSILON)
            w = v * r
            wd = d * gf_ref[0:1, :]
            dm = cot_ref[at, :].astype(F32) + r * (wd - w * jnp.mean(wd * w, axis=1, keepdims=True))
            dm_ref[...] = dm
            da_ref[...] = dm.astype(BF)

        d_middle, d_attn = call(
            norm_two_back,
            [((sub, width), F32), ((sub, width), BF)],
            ids,
            [middle, cot, gf, *dn_parts],
            vmem=8,
            name="norm_two_back",
        )
        d_attn_parts = plane_blocks(d_attn)

        def attend_back(ids_ref, info_ref, qs_ref, oa_ref, att_ref, wo_ref, *refs):
            d_refs, refs = refs[:n_plane], refs[n_plane:]
            kv_refs, refs = refs[:n_block], refs[n_block:]
            dq_ref, gwo_ref, dkv_refs = refs[0], refs[1], refs[2 : 2 + n_block]
            da_ref, do_ref, delta_ref, dqs_ref, acc_ref = refs[2 + n_block :]
            for b in range(n_plane):
                at = pl.multiple_of(plane_index(ids_ref, b) * sub, sub)
                da_ref[pl.ds(at, sub), :] = d_refs[b][...]
            low = lanes((rows, 128)) < 64
            do = nt_dot(da_ref[...], wo_ref[...]).astype(BF).astype(F32)
            first = jnp.where(low, 0.0, pltpu.roll(do, 64, 1))
            second = jnp.where(low, 0.0, do)
            do_ref[:rows, :] = first.astype(BF)
            do_ref[rows:, :] = second.astype(BF)
            delta_ref[:rows, :] = jnp.broadcast_to(
                jnp.sum(first * oa_ref[:rows, :], axis=1, keepdims=True), (rows, 128)
            )
            delta_ref[rows:, :] = jnp.broadcast_to(
                jnp.sum(second * oa_ref[rows:, :], axis=1, keepdims=True), (rows, 128)
            )
            dqs_ref[...] = jnp.zeros_like(dqs_ref)
            for k in range(n_block):
                grad = tn_dot(att_ref[...], da_ref[:, pl.ds(offset(ids_ref, k), wide)]).astype(BF)
                if blocks_mode:
                    gwo_ref[pl.ds(pl.multiple_of(owner(ids_ref, k) * q_cols, q_cols), q_cols), :] = grad
                else:
                    gwo_ref[...] = grad
                dkv_refs[k][...] = jnp.zeros_like(dkv_refs[k])

            def block(own, kv_ref, base, out_ref):
                kv = kv_ref[pl.ds(base, rows), :]
                acc_ref[...] = jnp.zeros_like(acc_ref)

                def body(c, carry):
                    at = pl.ds(pl.multiple_of(c * chunk, chunk), chunk)
                    q, d_out = qs_ref[at, :], do_ref[at, :]
                    p = masked_exp(ids_ref, info_ref, nt_dot(q, kv), c, own) * oa_ref[at, 0:1]
                    ds = (p * (nt_dot(d_out, kv) - delta_ref[at, 0:1])).astype(BF)
                    dqs_ref[at, :] += nn_dot(ds, kv)
                    acc_ref[...] += tn_dot(ds, q) + tn_dot(p.astype(BF), d_out)
                    return carry

                lax.fori_loop(0, 2 * rows // chunk, body, 0)
                out_ref[pl.ds(base, rows), :] = acc_ref[...].astype(BF)

            if blocks_mode:
                for k in range(n_block):
                    pl.when(owner(ids_ref, k) <= ids_ref[0])(
                        lambda k=k: block(owner(ids_ref, k), kv_refs[k], 0, dkv_refs[k])
                    )
            else:

                def step(j, carry):
                    block(j, kv_refs[0], pl.multiple_of(j * rows, rows), dkv_refs[0])
                    return carry

                lax.fori_loop(0, ids_ref[0] + 1, step, 0)
            dq_ref[...] = jnp.where(low, dqs_ref[:rows, :], pltpu.roll(dqs_ref[rows:, :], 64, 1))

        d_query, grad_out, *d_kv = call(
            attend_back,
            [((rows, 128), F32), ((n_block * q_cols, wide), BF)]
            + [((rows * (1 if blocks_mode else n_shard), 128), BF)] * n_block,
            ids,
            [row_info, queries, out_and_inverse, attended, own_rows, *d_attn_parts, *kv_parts],
            scratch=[
                pltpu.VMEM((rows, width), BF),
                pltpu.VMEM((2 * rows, 128), BF),
                pltpu.VMEM((2 * rows, 128), F32),
                pltpu.VMEM((2 * rows, 128), F32),
                pltpu.VMEM((rows, 128), F32),
            ],
            flops=10 * 2 * rows * rows * n_shard * 128,
            vmem=48,
            name="attend_back",
        )
        out_sum = lax.psum_scatter(
            grad_out, "shard", scatter_dimension=0 if blocks_mode else 1, tiled=True
        )
        if blocks_mode:
            d_kv_parts = [d_kv[0]] + [swap(d_kv[k], "shard", k) for k in range(1, n_block)]
        else:
            d_kv_parts = [lax.psum_scatter(d_kv[0], "shard", scatter_dimension=0, tiled=True)]

        def project_back(ids_ref, x_ref, n_ref, raw_ref, dq_ref, cos_ref, sin_ref, hg_ref, gp_ref, *refs):
            dkv_refs, refs = refs[:n_block], refs[n_block:]
            w_refs, refs = refs[:n_block], refs[n_block:]
            send_ref, keep_ref, g_refs = refs[0], refs[1], refs[2 : 2 + n_block]
            low_ref, r_ref = refs[-2:]
            lane = lanes((rows, 128))
            low, first = lane < 64, (lane % 64) < 32
            cos, sin = cos_ref[...], sin_ref[...]

            def back(v, g, d):
                d = d * cos + turn_back(d * sin, first)
                r = lax.rsqrt(head_mean(v * v, low) + EPSILON)
                w = v * r
                wd = d * g
                return r * (wd - w * head_mean(wd * w, low)), jnp.sum(d * w, axis=0, keepdims=True)

            scale = 1.0 / math.sqrt(head)
            dq, gain_q = back(raw_ref[:, :128], hg_ref[0:1, :], dq_ref[...] * scale)
            dkv = tree([p[...].astype(F32) for p in dkv_refs])
            dk, gain_k = back(raw_ref[:, 128:], hg_ref[8:9, :], dkv)
            low_ref[:, :128] = dq.astype(BF)
            low_ref[:, 128:] = jnp.where(low, dk, dkv).astype(BF)
            gain_q = gain_q + pltpu.roll(jnp.broadcast_to(gain_q, (8, 128)), 64, 1)[0:1]
            head_row = jnp.where(low[0:1], gain_q, pltpu.roll(jnp.broadcast_to(gain_k, (8, 128)), 64, 1)[0:1])
            head_row = jnp.concatenate([head_row, jnp.zeros((1, wide - 128), F32)], axis=1)
            x = x_ref[...].astype(F32)
            r_ref[...] = jnp.broadcast_to(
                lax.rsqrt(jnp.mean(x * x, axis=1, keepdims=True) + EPSILON), (rows, 128)
            )
            for k in range(n_block):
                cols = pl.ds(offset(ids_ref, k), wide)
                g_refs[k][:wide, :] = tn_dot(n_ref[:, cols], low_ref[...]).astype(BF)
                dn = nt_dot(low_ref[...], w_refs[k][:wide, :])
                low_dn = dn.astype(BF)
                for c in range(n_heads):
                    part = low_dn[c * half : (c + 1) * half]

                    @pl.when(c == ids_ref[1])
                    def _():
                        keep_ref[:, cols] = part

                    @pl.when(c != ids_ref[1])
                    def _():
                        send_ref[:, cols] = part

                w = x_ref[:, cols].astype(F32) * r_ref[:, 0:1]
                three = [jnp.sum(dn * w, axis=0, keepdims=True), gp_ref[0:1, cols], head_row]
                if blocks_mode:
                    high = [v.astype(BF).astype(F32) for v in three]
                    rest = [a - b for a, b in zip(three, high)]
                    packed_rows = high + rest + [jnp.zeros((GAIN_ROWS - 6, wide), F32)]
                    g_refs[k][wide:, :] = jnp.concatenate(packed_rows, axis=0).astype(BF)
                else:
                    refs[3][...] = jnp.concatenate(three + [jnp.zeros((5, wide), F32)], axis=0)

        if blocks_mode:
            grad_shapes = [((wide + GAIN_ROWS, 256), BF)] * n_block
        else:
            grad_shapes = [((wide, 256), BF), ((8, width), F32)]
        results = call(
            project_back,
            [((half, width), BF), ((half, width), BF)] + grad_shapes,
            ids,
            [block_input, normed_one, raw, d_query, cosine, sine, head_gains, ffn_gain_part, *d_kv_parts, *qkv_parts],
            scratch=[pltpu.VMEM((rows, 256), BF), pltpu.VMEM((rows, 128), F32)],
            flops=2 * rows * width * 512,
            vmem=32,
            name="project_back",
        )
        d1_send, d1_keep, grads = results[0], results[1], results[2:]
        d1_parts = plane_sum_parts(d1_keep, d1_send)
        def norm_one_back(ids_ref, x_ref, dm_ref, ga_ref, *refs):
            part_refs, ig_ref = refs[:n_tensor], refs[n_tensor]
            at = pl.ds(pl.multiple_of((ids_ref[1] * n_tensor + ids_ref[2]) * sub, sub), sub)
            d = tree([p[...].astype(F32) for p in part_refs])
            v = x_ref[at, :].astype(F32)
            r = lax.rsqrt(jnp.mean(v * v, axis=1, keepdims=True) + EPSILON)
            w = v * r
            wd = d * ga_ref[0:1, :]
            back = r * (wd - w * jnp.mean(wd * w, axis=1, keepdims=True))
            ig_ref[...] = (dm_ref[...] + back).astype(BF)

        (input_block,) = call(
            norm_one_back,
            [((sub, width), BF)],
            ids,
            [block_input, d_middle, ga, *d1_parts],
            vmem=8,
            name="norm_one_back",
        )
        input_parts = plane_blocks(input_block)

        def stack_rows(ids_ref, *refs):
            for b in range(n_plane):
                at = pl.multiple_of(plane_index(ids_ref, b) * sub, sub)
                refs[-1][pl.ds(at, sub), :] = refs[b][...].astype(F32)

        (input_grad,) = call(
            stack_rows, [((rows, width), F32)], ids, input_parts, vmem=8, name="stack_rows"
        )

        def place(ids_ref, *refs):
            b_refs, (q_ref, k_ref, v_ref, o_ref, s_ref) = refs[:n_tensor], refs[n_tensor:]
            for k in range(n_tensor):
                s_ref[ids_ref[2] ^ k] = b_refs[k][...].astype(F32)
            low = lanes((depth, 128)) < 64
            for i in range(n_tensor):
                q_ref[:, i * 128 : (i + 1) * 128] = s_ref[i, :depth, :128]
                o_ref[i * q_cols : (i + 1) * q_cols, :] = s_ref[i, depth + GAIN_ROWS :, :]
            for i in range(n_tensor // 2):
                even, odd = s_ref[2 * i, :depth, 128:], s_ref[2 * i + 1, :depth, 128:]
                k_ref[:, i * 128 : (i + 1) * 128] = jnp.where(low, even, pltpu.roll(odd, 64, 1))
                v_ref[:, i * 128 : (i + 1) * 128] = jnp.where(low, pltpu.roll(even, 64, 1), odd)

        if blocks_mode:
            sums = [grads[0]] + [swap(grads[k], "shard", k) for k in range(1, n_block)]
            own_sum = tree([s.astype(F32) for s in sums]).astype(BF)
            bundle = jnp.concatenate([own_sum, out_sum], axis=0)
            bundles = [bundle] + [swap(bundle, "tensor", k) for k in range(1, n_tensor)]
            total = tree([b[depth : depth + GAIN_ROWS].astype(F32) for b in bundles])
            total = total + swap(total, "heads", 1)
            total = total[0:3] + total[3:6]
            attn_gain_grad, ffn_gain_grad, head_gain_grad = total[0], total[1], total[2]
            query_grad, key_grad, value_grad, out_weight_grad = call(
                place,
                [
                    ((depth, n_tensor * q_cols), F32),
                    ((depth, n_tensor * k_cols), F32),
                    ((depth, n_tensor * k_cols), F32),
                    ((n_tensor * q_cols, depth), F32),
                ],
                ids,
                bundles,
                scratch=[pltpu.VMEM((n_tensor,) + bundle.shape, F32)],
                vmem=16,
                name="place",
            )
        else:
            own_sum = lax.psum_scatter(grads[0], "shard", scatter_dimension=0, tiled=True)
            total = lax.psum(grads[1], ("shard", "heads", "tensor"))
            attn_gain_grad = lax.dynamic_slice_in_dim(total[0], z * depth, depth)
            ffn_gain_grad = lax.dynamic_slice_in_dim(total[1], z * depth, depth)
            head_gain_grad = total[2]
            found = lax.all_gather(own_sum, "tensor", axis=0).astype(F32)
            flat = lambda x: jnp.swapaxes(x, 0, 1).reshape(depth, -1)
            query_grad = flat(found[:, :, :128])
            key_grad, value_grad = flat(found[:, :, 128:192]), flat(found[:, :, 192:])
            out_weight_grad = lax.all_gather(out_sum, "tensor", axis=0, tiled=True).astype(F32)

        other = swap(gate_up_sum, "heads", 1)
        lower = jnp.where(first_core, gate_up_sum, other)
        upper = jnp.where(first_core, other, gate_up_sum)
        gate_grad = jnp.concatenate([lower[:, :hid], upper[:, :hid]], axis=1).astype(F32)
        up_grad = jnp.concatenate([lower[:, hid:], upper[:, hid:]], axis=1).astype(F32)
        other = swap(down_sum, "heads", 1)
        lower = jnp.where(first_core, down_sum, other)
        upper = jnp.where(first_core, other, down_sum)
        down_grad = jnp.concatenate([lower, upper], axis=0).astype(F32)
        return (
            block_output,
            input_grad,
            attn_gain_grad,
            query_grad,
            key_grad,
            value_grad,
            head_gain_grad[:head],
            head_gain_grad[head : 2 * head],
            out_weight_grad,
            ffn_gain_grad,
            gate_grad,
            up_grad,
            down_grad,
        )

    return on_device


def solution(mesh):
    placed = (
        P("shard", None),
        P("shard"),
        P("shard", "heads"),
        P("shard", "heads"),
        P("shard", "heads"),
        P(),
        P(),
        P("heads", "shard"),
        P("shard"),
        P("shard", "tensor"),
        P("shard", "tensor"),
        P("tensor", "shard"),
        P(),
        P(),
        P("shard", None),
    )
    return jax.shard_map(
        make(mesh),
        mesh=mesh,
        in_specs=placed,
        out_specs=(
            P("shard", None),
            P("shard", None),
            P("shard"),
            P("shard", "heads"),
            P("shard", "heads"),
            P("shard", "heads"),
            P(),
            P(),
            P("heads", "shard"),
            P("shard"),
            P("shard", "tensor"),
            P("shard", "tensor"),
            P("tensor", "shard"),
        ),
        check_vma=False,
    )
```

```python
import math

import jax
import jax.numpy as jnp
import numpy as np
from jax import lax
from jax.experimental import pallas as pl
from jax.experimental.pallas import tpu as pltpu
from jax.sharding import PartitionSpec as P

EPSILON = 1e-05
ROPE_THETA = 1000000.0
BF = jnp.bfloat16
F32 = jnp.float32
MIB = 1 << 20
GAIN_ROWS = 16
ROUTE_A = [(0, 1), (1, 3), (2, 0), (3, 2)]
ROUTE_B = [(0, 2), (1, 0), (2, 3), (3, 1)]


def nn_dot(a, b):
    return lax.dot_general(a, b, (((1,), (0,)), ((), ())), preferred_element_type=F32)


def nt_dot(a, b):
    return lax.dot_general(a, b, (((1,), (1,)), ((), ())), preferred_element_type=F32)


def tn_dot(a, b):
    return lax.dot_general(a, b, (((0,), (0,)), ((), ())), preferred_element_type=F32)


def call(kernel, outs, ids, arrays, scratch=(), vmem=32, flops=0, name=None, n_hbm=0):
    shapes = [jax.ShapeDtypeStruct(s, d) for s, d in outs]
    moved = sum(a.size * a.dtype.itemsize for a in arrays)
    moved += sum(math.prod(s.shape) * s.dtype.itemsize for s in shapes)
    return pl.pallas_call(
        kernel,
        out_shape=shapes,
        in_specs=[pl.BlockSpec(memory_space=pltpu.SMEM)]
        + [pl.BlockSpec(memory_space=pltpu.HBM) for _ in range(n_hbm)]
        + [pl.BlockSpec(memory_space=pltpu.VMEM) for _ in arrays[n_hbm:]],
        out_specs=[pl.BlockSpec(memory_space=pltpu.VMEM) for _ in shapes],
        scratch_shapes=list(scratch),
        compiler_params=pltpu.CompilerParams(vmem_limit_bytes=vmem * MIB),
        cost_estimate=pl.CostEstimate(flops=int(flops), bytes_accessed=int(moved), transcendentals=0),
        name=name,
    )(ids, *arrays)


def lanes(shape):
    return lax.broadcasted_iota(jnp.int32, shape, 1)


def head_mean(v, low):
    first = jnp.sum(jnp.where(low, v, 0.0), axis=1, keepdims=True)
    second = jnp.sum(jnp.where(low, 0.0, v), axis=1, keepdims=True)
    return jnp.where(low, first, second) * (1.0 / 64.0)


def turn(v, first):
    return jnp.where(first, -pltpu.roll(v, 96, 1), pltpu.roll(v, 32, 1))


def turn_back(v, first):
    return jnp.where(first, pltpu.roll(v, 96, 1), -pltpu.roll(v, 32, 1))


def tree(values, dtype=F32):
    values = [v.astype(F32) for v in values]
    while len(values) > 1:
        pairs = [values[i] + values[i + 1] for i in range(0, len(values) - 1, 2)]
        values = pairs + values[len(values) - len(values) % 2 :]
    return values[0].astype(dtype)


def make(mesh):
    n_shard, n_heads, n_tensor = (mesh.shape[a] for a in ("shard", "heads", "tensor"))
    blocks_mode = n_shard == 4
    n_plane = n_heads * n_tensor

    def swap(x, axis, k):
        size = mesh.shape[axis]
        return lax.ppermute(x, axis, [(i, i ^ k) for i in range(size)])

    def route(x, pairs, back):
        return lax.ppermute(x, "shard", [(b, a) for a, b in pairs] if back else pairs)

    def inner():
        z = lax.axis_index("shard")
        return (z == 1) | (z == 2)

    def shard_blocks(x):
        return [x, route(x, ROUTE_A, False), route(x, ROUTE_B, False), swap(x, "shard", 3)]

    def after(values, *first):
        return lax.optimization_barrier((*values, *first))[: len(values)]

    def shard_sum(blocks):
        a, b = route(blocks[1], ROUTE_A, True), route(blocks[2], ROUTE_B, True)
        near, far = jnp.where(inner(), b, a), jnp.where(inner(), a, b)
        return tree([blocks[0], near, far, swap(blocks[3], "shard", 3)], BF)

    def shard_sum_staged(blocks, later):
        (found,) = after((swap(blocks[3], "shard", 1),), later)
        found = found.astype(F32)
        a = (blocks[1].astype(F32) + jnp.where(inner(), 0.0, found)).astype(BF)
        b = (blocks[2].astype(F32) + jnp.where(inner(), found, 0.0)).astype(BF)
        return blocks[0], route(a, ROUTE_A, True), b

    def plane_blocks(x):
        same = [x] + [swap(x, "tensor", k) for k in range(1, n_tensor)]
        found = list(same)
        for i in range(1, n_heads):
            found += [swap(s, "heads", i) for s in same]
        return found

    def plane_index(ids, b):
        return (ids[1] ^ (b // n_tensor)) * n_tensor + (ids[2] ^ (b % n_tensor))

    def on_device(
        block_input,
        attn_gain,
        query_weight,
        key_weight,
        value_weight,
        query_gain,
        key_gain,
        output_weight,
        ffn_gain,
        gate_weight,
        up_weight,
        down_weight,
        lengths,
        packing,
        out_grad,
    ):
        rows, width = block_input.shape
        depth = query_weight.shape[0]
        head = query_gain.shape[0]
        hidden_all = gate_weight.shape[1]
        hid = hidden_all // n_heads
        q_cols = query_weight.shape[1] // n_tensor
        k_cols = key_weight.shape[1] // n_tensor
        n_block = n_shard if blocks_mode else 1
        wide = width // n_block
        padded = -(-hid // 128) * 128
        whole = 2 * hid
        sub = rows // n_plane
        half = rows // n_heads
        step = half
        z, h, t = (lax.axis_index(a) for a in ("shard", "heads", "tensor"))
        if blocks_mode:
            ids = jnp.stack([z, h, t, z, z ^ jnp.where(inner(), 1, 2), z ^ jnp.where(inner(), 2, 1), z ^ 3])
        else:
            ids = jnp.stack([z, h, t])
        ids = ids.astype(jnp.int32)

        def owner(ids_ref, k):
            return ids_ref[3 + k]

        def offset(ids_ref, k):
            return pl.multiple_of(owner(ids_ref, k) * wide, wide) if blocks_mode else 0

        def fetch(pairs, sems):
            copies = [pltpu.make_async_copy(a, b, sems.at[i]) for i, (a, b) in enumerate(pairs)]
            for copy in copies:
                copy.start()
            return copies

        def share_attn(ids_ref, q_hbm, k_hbm, v_hbm, o_hbm, ag_hbm, fg_hbm, *outs):
            own_ref = outs[0]
            q_ref, k_ref, v_ref, ag_ref, fg_ref, sems = outs[-6:]
            i = ids_ref[2]
            tile = pl.ds(pl.multiple_of((i // 2) * 128, 128), 128)
            at = pl.multiple_of(i * q_cols, q_cols)
            out_ref = own_ref.at[depth + GAIN_ROWS :, :] if blocks_mode else outs[2]
            copies = fetch(
                [
                    (ag_hbm, ag_ref),
                    (fg_hbm, fg_ref),
                    (q_hbm.at[:, pl.ds(at, q_cols)], q_ref),
                    (k_hbm.at[:, tile], k_ref),
                    (v_hbm.at[:, tile], v_ref),
                    (o_hbm.at[pl.ds(at, q_cols), :], out_ref),
                ],
                sems,
            )
            for copy in copies:
                copy.wait()
            both = [ag_ref[...].astype(F32).reshape(1, depth), fg_ref[...].astype(F32).reshape(1, depth)]
            both = jnp.concatenate(both + [jnp.zeros((GAIN_ROWS - 2, depth), F32)], axis=0).astype(BF)
            if blocks_mode:
                own_ref[depth : depth + GAIN_ROWS, :] = both
            else:
                outs[1][...] = both
            own_ref[:depth, :128] = q_ref[...]
            k_, v_ = k_ref[...].astype(F32), v_ref[...].astype(F32)
            even = (i % 2) == 0
            low = lanes((depth, 128)) < 64
            k_ = jnp.where(even, k_, pltpu.roll(k_, 64, 1))
            v_ = jnp.where(even, pltpu.roll(v_, 64, 1), v_)
            own_ref[:depth, 128:] = jnp.where(low, k_, v_).astype(BF)

        if blocks_mode:
            share_shapes = [((depth + GAIN_ROWS + q_cols, 256), BF)]
        else:
            share_shapes = [((depth, 256), BF), ((GAIN_ROWS, depth), BF), ((q_cols, depth), BF)]
        own_attn, *own_more = call(
            share_attn,
            share_shapes,
            ids,
            [query_weight, key_weight, value_weight, output_weight, attn_gain, ffn_gain],
            scratch=[pltpu.VMEM((depth, 128), BF)] * 3
            + [pltpu.VMEM((depth,), BF)] * 2
            + [pltpu.SemaphoreType.DMA((6,))],
            vmem=56,
            n_hbm=6,
            name="share_attn",
        )

        def share_ffn(ids_ref, g_hbm, u_hbm, d_hbm, own_ref, g_ref, u_ref, sems):
            rows_ = pl.ds(pl.multiple_of(ids_ref[1] * hid, 16), hid)
            pairs = [(g_hbm, g_ref), (u_hbm, u_ref), (d_hbm.at[rows_, :], own_ref.at[whole:, :])]
            for copy in fetch(pairs, sems):
                copy.wait()
            for i, ref in enumerate((g_ref, u_ref)):
                part = ref[...].astype(F32)
                part = jnp.where(ids_ref[1] == 0, part, pltpu.roll(part, hid, 1))[:, :padded]
                own_ref[i * hid : (i + 1) * hid, :] = part.T[:hid].astype(BF)

        (own_ffn,) = call(
            share_ffn,
            [((whole + hid, depth), BF)],
            ids,
            [gate_weight, up_weight, down_weight],
            scratch=[
                pltpu.VMEM((depth, whole), BF),
                pltpu.VMEM((depth, whole), BF),
                pltpu.SemaphoreType.DMA((3,)),
            ],
            vmem=8,
            n_hbm=3,
            name="share_ffn",
        )

        count = lengths.shape[0]
        frequency = np.power(np.float64(ROPE_THETA), -np.arange(head // 2) * (2.0 / head))
        frequency = jnp.asarray(np.tile(frequency, 4)[None].astype(np.float32))

        def layout(ids_ref, len_hbm, pack_hbm, freq_hbm, qg_hbm, kg_hbm, *refs):
            info_ref, angle_ref, hg_ref, len_ref, pack_ref, freq_ref, qg_ref, kg_ref, sems = refs
            pairs = [(len_hbm, len_ref), (pack_hbm, pack_ref), (freq_hbm, freq_ref), (qg_hbm, qg_ref), (kg_hbm, kg_ref)]
            for copy in fetch(pairs, sems):
                copy.wait()
            token = ids_ref[0] * rows + lax.broadcasted_iota(jnp.int32, (rows, 128), 0)
            start = jnp.zeros((rows, 128), jnp.int32)
            end = jnp.int32(0)
            for j in range(count):
                end = end + len_ref[pack_ref[j]]
                start = jnp.where(token >= end, end, start)
            live = token < end
            lowest = jnp.where(live, start, token).astype(F32)
            info_ref[...] = jnp.where(lanes((rows, 128)) == 0, lowest, live.astype(F32))
            angle_ref[...] = (token - start).astype(F32) * freq_ref[...]
            q, k_ = qg_ref[...].astype(F32).reshape(1, head), kg_ref[...].astype(F32).reshape(1, head)
            q = jnp.concatenate([q, q], axis=1)
            k_ = jnp.concatenate([k_, jnp.ones((1, head), F32)], axis=1)
            hg_ref[:8, :] = jnp.broadcast_to(q, (8, 128))
            hg_ref[8:, :] = jnp.broadcast_to(k_, (8, 128))

        row_info, angles, head_gains = call(
            layout,
            [((rows, 128), F32), ((rows, 128), F32), ((16, 128), F32)],
            ids,
            [lengths, packing, frequency, query_gain, key_gain],
            scratch=[
                pltpu.SMEM((count,), jnp.int32),
                pltpu.SMEM((count,), jnp.int32),
                pltpu.VMEM((1, 128), F32),
                pltpu.VMEM((head,), BF),
                pltpu.VMEM((head,), BF),
                pltpu.SemaphoreType.DMA((5,)),
            ],
            vmem=2,
            n_hbm=5,
            name="layout",
        )
        cosine, sine = jnp.cos(angles), jnp.sin(angles)

        if blocks_mode:
            attn_parts = shard_blocks(own_attn)
            gain_parts = []
        else:
            gather = lambda x, axis: [lax.all_gather(x, "shard", axis=axis, tiled=True)]
            attn_parts = gather(own_attn, 0)
            gain_parts = gather(own_more[0], 1)
            out_parts = gather(own_more[1], 1)
            ffn_parts = gather(own_ffn, 1)

        def project(ids_ref, x_ref, cos_ref, sin_ref, hg_ref, *refs):
            w_refs, refs = refs[:n_block], refs[n_block:]
            g_refs, refs = refs[: len(gain_parts)], refs[len(gain_parts) :]
            n_ref, raw_ref, qs_ref, kv_ref, ga_ref, gf_ref = refs
            for k in range(n_block):
                both = (g_refs[0][...] if g_refs else w_refs[k][wide : wide + GAIN_ROWS, :]).astype(F32)
                where = pl.ds(offset(ids_ref, k), wide)
                ga_ref[:, where] = jnp.broadcast_to(both[0:1], (8, wide))
                gf_ref[:, where] = jnp.broadcast_to(both[1:2], (8, wide))
            step = 128

            def body(c, carry):
                at = pl.ds(pl.multiple_of(c * step, step), step)
                x = x_ref[at, :].astype(F32)
                r = lax.rsqrt(jnp.mean(x * x, axis=1, keepdims=True) + EPSILON)
                n_ref[at, :] = (x * r * ga_ref[0:1, :]).astype(BF)
                acc = jnp.zeros((step, 256), F32)
                for k in range(n_block):
                    acc += nn_dot(n_ref[at, pl.ds(offset(ids_ref, k), wide)], w_refs[k][:wide, :])
                raw_ref[at, :] = acc
                lane = lanes((step, 128))
                low, first = lane < 64, (lane % 64) < 32
                cos, sin = cos_ref[at, :], sin_ref[at, :]
                q, kv = acc[:, :128], acc[:, 128:]
                q = q * lax.rsqrt(head_mean(q * q, low) + EPSILON) * hg_ref[0:1, :]
                q = (q * cos + turn(q, first) * sin).astype(BF).astype(F32) * (1.0 / math.sqrt(head))
                qs_ref[at, :] = jnp.where(low, q, 0.0).astype(BF)
                qs_ref[pl.ds(pl.multiple_of(rows + c * step, step), step), :] = jnp.where(
                    low, pltpu.roll(q, 64, 1), 0.0
                ).astype(BF)
                k_ = kv * lax.rsqrt(head_mean(kv * kv, low) + EPSILON) * hg_ref[8:9, :]
                k_ = k_ * cos + turn(k_, first) * sin
                kv_ref[at, :] = jnp.where(low, k_, kv).astype(BF)
                return carry

            lax.fori_loop(0, rows // step, body, 0)

        normed_one, raw, queries, own_kv, ga, gf = call(
            project,
            [
                ((rows, width), BF),
                ((rows, 256), F32),
                ((2 * rows, 128), BF),
                ((rows, 128), BF),
                ((8, width), F32),
                ((8, width), F32),
            ],
            ids,
            [block_input, cosine, sine, head_gains, *attn_parts, *gain_parts],
            flops=2 * rows * width * 256,
            vmem=4,
            name="project",
        )
        if blocks_mode:
            kv_parts = shard_blocks(own_kv)
            (own_ffn,) = after((own_ffn,), *kv_parts[1:])
            ffn_a, ffn_b = route(own_ffn, ROUTE_A, False), route(own_ffn, ROUTE_B, False)
        else:
            kv_parts = [lax.all_gather(own_kv, "shard", axis=0, tiled=True)]

        if blocks_mode:

            def beside(ids_ref, *refs):
                for k in range(n_block):
                    refs[-1][:, pl.ds(offset(ids_ref, k), wide)] = refs[k][wide + GAIN_ROWS :, :]

            late = after(attn_parts, *kv_parts[1:])
            (own_rows,) = call(beside, [((q_cols, width), BF)], ids, late, vmem=1, name="beside")
        else:
            own_rows = out_parts[0]
        row_parts = [own_rows] + [swap(own_rows, "tensor", k) for k in range(1, n_tensor)]

        def below(ids_ref, *refs):
            for k in range(n_tensor):
                at = pl.multiple_of((ids_ref[2] ^ k) * q_cols, q_cols)
                refs[-1][pl.ds(at, q_cols), :] = refs[k][...]

        (out_half,) = call(
            below, [((n_tensor * q_cols, width), BF)], ids, row_parts, vmem=1, name="below"
        )
        out_halves = [out_half, swap(out_half, "heads", 1)]

        chunk = 256

        def over_keys(ids_ref, kv_refs, block):
            if blocks_mode:
                for k in range(n_block):
                    pl.when(owner(ids_ref, k) <= ids_ref[0])(
                        lambda k=k: block(owner(ids_ref, k), kv_refs[k], 0)
                    )
            else:

                def step(j, carry):
                    block(j, kv_refs[0], pl.multiple_of(j * rows, rows))
                    return carry

                lax.fori_loop(0, ids_ref[0] + 1, step, 0)

        def masked_exp(ids_ref, info_ref, score, c, own):
            row = (c * chunk) % rows
            at = pl.ds(pl.multiple_of(row, chunk), chunk)
            col = lanes((chunk, rows))
            lowest_ = info_ref[at, 0:1].astype(jnp.int32) - own * rows
            mine = lax.broadcasted_iota(jnp.int32, (chunk, 1), 0) + (row + (ids_ref[0] - own) * rows)
            return jnp.where((col >= lowest_) & (col <= mine), jnp.exp(score), 0.0)

        def attend(ids_ref, info_ref, qs_ref, *refs):
            kv_refs, (att_ref, oa_ref, acc_ref) = refs[:n_block], refs[n_block:]
            acc_ref[...] = jnp.zeros_like(acc_ref)
            low = lanes((rows, 128)) < 64

            def block(own, kv_ref, base):
                kv = kv_ref[pl.ds(base, rows), :]
                counted = jnp.where(low, 1.0, kv.astype(F32)).astype(BF)

                def body(c, carry):
                    at = pl.ds(pl.multiple_of(c * chunk, chunk), chunk)
                    p = masked_exp(ids_ref, info_ref, nt_dot(qs_ref[at, :], kv), c, own)
                    acc_ref[at, :] += nn_dot(p.astype(BF), counted)
                    return carry

                lax.fori_loop(0, 2 * rows // chunk, body, 0)

            over_keys(ids_ref, kv_refs, block)
            for i in range(2):
                acc = acc_ref[i * rows : (i + 1) * rows, :]
                inverse = 1.0 / jnp.where(low, acc, 1.0)
                done = jnp.where(low, inverse, acc * pltpu.roll(inverse, 64, 1))
                oa_ref[i * rows : (i + 1) * rows, :] = done
            att_ref[...] = jnp.where(
                low, pltpu.roll(oa_ref[:rows, :], 64, 1), oa_ref[rows:, :]
            ).astype(BF)

        attended, out_and_inverse = call(
            attend,
            [((rows, 128), BF), ((2 * rows, 128), F32)],
            ids,
            [row_info, queries, *kv_parts],
            scratch=[pltpu.VMEM((2 * rows, 128), F32)],
            flops=4 * 2 * rows * rows * n_shard * 128,
            vmem=4,
            name="attend",
        )
        attended_parts = plane_blocks(attended)

        def my_rows(ids_ref):
            return pl.ds(pl.multiple_of((ids_ref[1] * n_tensor + ids_ref[2]) * sub, sub), sub)

        def middle_part(ids_ref, x_ref, gf_ref, *refs):
            wo_refs, refs = refs[:n_heads], refs[n_heads:]
            a_refs, (n2_ref, mid_ref, a_ref, m_ref) = refs[:n_plane], refs[n_plane:]
            deep = n_tensor * q_cols
            for b in range(n_plane):
                at = pl.multiple_of(plane_index(ids_ref, b) * q_cols, q_cols)
                a_ref[:, pl.ds(at, q_cols)] = a_refs[b][...]

            def body(c, carry):
                at = pl.ds(pl.multiple_of(c * step, step), step)
                parts = [
                    nn_dot(a_ref[at, pl.ds(pl.multiple_of((ids_ref[1] ^ i) * deep, deep), deep)], wo_refs[i][...])
                    for i in range(n_heads)
                ]
                middle = x_ref[at, :].astype(F32) + tree(parts)
                m_ref[at, :] = middle
                r = lax.rsqrt(jnp.mean(middle * middle, axis=1, keepdims=True) + EPSILON)
                n2_ref[at, :] = (middle * r * gf_ref[0:1, :]).astype(BF)
                return carry

            lax.fori_loop(0, n_heads, body, 0)
            mid_ref[...] = m_ref[my_rows(ids_ref), :]

        normed_two, middle = call(
            middle_part,
            [((rows, width), BF), ((sub, width), F32)],
            ids,
            [block_input, gf, *out_halves, *attended_parts],
            scratch=[pltpu.VMEM((rows, width), BF), pltpu.VMEM((rows, width), F32)],
            flops=2 * rows * width * width,
            vmem=8,
            name="middle",
        )

        if blocks_mode:
            (chosen,) = after((jnp.where(inner(), ffn_b, ffn_a),), *attended_parts[1:n_tensor])
            ffn_parts = [own_ffn, ffn_a, ffn_b, swap(chosen, "shard", 1)]

        def feed_forward(ids_ref, info_ref, og_ref, n2_ref, *refs):
            w_refs, refs = refs[:n_block], refs[n_block:]
            send_ref, keep_ref, fo_send_ref, fo_keep_ref, dg_ref, du_ref, hid_ref, cot_ref, both_ref = refs

            def body(c, carry):
                at = pl.ds(pl.multiple_of(c * step, step), step)
                cot_ref[at, :] = (og_ref[at, :].astype(F32) * info_ref[at, 1:2]).astype(BF)
                gate = up = dh = jnp.zeros((step, hid), F32)
                for k in range(n_block):
                    cols = pl.ds(offset(ids_ref, k), wide)
                    gate += nt_dot(n2_ref[at, cols], w_refs[k][:hid, :])
                    up += nt_dot(n2_ref[at, cols], w_refs[k][hid:whole, :])
                    dh += nt_dot(cot_ref[at, cols], w_refs[k][whole:, :])
                sig = 1.0 / (1.0 + jnp.exp(-gate))
                act = gate * sig
                hid_ref[at, :] = (act * up).astype(BF)
                dg_ref[at, :] = (dh * up * sig * (1.0 + gate * (1.0 - sig))).astype(BF)
                du_ref[at, :] = (dh * act).astype(BF)
                for k in range(n_block):
                    off = offset(ids_ref, k)
                    dn = nn_dot(dg_ref[at, :], w_refs[k][:hid, :]) + nn_dot(du_ref[at, :], w_refs[k][hid:whole, :])
                    both_ref[:, pl.ds(off, wide)] = dn.astype(BF)
                    off = pl.multiple_of(width + off, wide)
                    both_ref[:, pl.ds(off, wide)] = nn_dot(hid_ref[at, :], w_refs[k][whole:, :]).astype(BF)

                @pl.when(c == ids_ref[1])
                def _():
                    keep_ref[...] = both_ref[:, :width]
                    fo_keep_ref[...] = both_ref[:, width:]

                @pl.when(c != ids_ref[1])
                def _():
                    send_ref[...] = both_ref[:, :width]
                    fo_send_ref[...] = both_ref[:, width:]

                return carry

            lax.fori_loop(0, n_heads, body, 0)

        dn_send, dn_keep, fo_send, fo_keep, d_gate, d_up, hidden, cot = call(
            feed_forward,
            [
                ((half, width), BF),
                ((half, width), BF),
                ((half, width), BF),
                ((half, width), BF),
                ((rows, hid), BF),
                ((rows, hid), BF),
                ((rows, hid), BF),
                ((rows, width), BF),
            ],
            ids,
            [row_info, out_grad, normed_two, *ffn_parts],
            scratch=[pltpu.VMEM((half, 2 * width), BF)],
            flops=2 * rows * width * 6 * hid,
            vmem=14,
            name="feed_forward",
        )

        def split(ids_ref, keep_ref, got_ref, *outs):
            for k in range(n_tensor):
                at = pl.ds(pl.multiple_of((ids_ref[2] ^ k) * sub, sub), sub)
                total = keep_ref[at, :].astype(F32) + got_ref[at, :].astype(F32)
                outs[k][...] = total.astype(BF)

        def plane_halves(keep, send):
            got = swap(send, "heads", 1)
            return call(split, [((sub, width), BF)] * n_tensor, ids, [keep, got], vmem=2, name="split")

        def plane_sum_parts(parts):
            return [parts[0]] + [swap(parts[k], "tensor", k) for k in range(1, n_tensor)]

        dn_parts = plane_sum_parts(plane_halves(dn_keep, dn_send))

        def ffn_grads(ids_ref, n2_ref, cot_ref, dg_ref, du_ref, hid_ref, *outs):
            outs, turned_ref = outs[:-1], outs[-1]
            for i, ref in enumerate((dg_ref, du_ref, hid_ref)):
                turned_ref[i * hid : (i + 1) * hid, :] = ref[...].T
            for k in range(n_block):
                cols = pl.ds(offset(ids_ref, k), wide)
                outs[k][:whole, :] = nn_dot(turned_ref[:whole, :], n2_ref[:, cols]).astype(BF)
                outs[k][whole:, :] = nn_dot(turned_ref[whole:, :], cot_ref[:, cols]).astype(BF)

        grad_ffn = call(
            ffn_grads,
            [((whole + hid, wide), BF)] * n_block,
            ids,
            [normed_two, cot, d_gate, d_up, hidden],
            scratch=[pltpu.VMEM((whole + hid, rows), BF)],
            flops=2 * rows * width * 3 * hid,
            vmem=8,
            name="ffn_grads",
        )
        (first_part,) = after((dn_parts[0],), grad_ffn[0])
        dn_parts = [first_part] + dn_parts[1:]

        def norm_two_back(ids_ref, mid_ref, cot_ref, gf_ref, *refs):
            part_refs, (dm_ref, da_ref, gp_ref) = refs[:n_tensor], refs[n_tensor:]
            d = tree([p[...] for p in part_refs])
            v = mid_ref[...]
            r = lax.rsqrt(jnp.mean(v * v, axis=1, keepdims=True) + EPSILON)
            w = v * r
            wd = d * gf_ref[0:1, :]
            cot_ = cot_ref[my_rows(ids_ref), :].astype(F32)
            dm = cot_ + r * (wd - w * jnp.mean(wd * w, axis=1, keepdims=True))
            dm_ref[...] = dm
            da_ref[...] = dm.astype(BF)
            gp_ref[...] = jnp.broadcast_to(jnp.sum(d * w, axis=0, keepdims=True), gp_ref.shape)

        d_middle, d_attn, ffn_gain_part = call(
            norm_two_back,
            [((sub, width), F32), ((sub, width), BF), ((8, width), F32)],
            ids,
            [middle, cot, gf, *dn_parts],
            vmem=4,
            name="norm_two_back",
        )
        if blocks_mode:
            ffn_own, first_route, second_route = shard_sum_staged(grad_ffn, d_attn)
        else:
            ffn_sum = lax.psum_scatter(grad_ffn[0], "shard", scatter_dimension=1, tiled=True)
        row_blocks = plane_blocks(d_attn)
        fo_halves = plane_halves(fo_keep, after((fo_send,), d_attn)[0])

        def attend_back(ids_ref, info_ref, qs_ref, oa_ref, wo_ref, *refs):
            d_refs, refs = refs[:n_plane], refs[n_plane:]
            kv_refs, refs = refs[:n_block], refs[n_block:]
            dq_ref, da_ref, dkv_refs = refs[0], refs[1], refs[2 : 2 + n_block]
            do_ref, delta_ref, dqs_ref, acc_ref = refs[2 + n_block :]
            for b in range(n_plane):
                at = pl.multiple_of(plane_index(ids_ref, b) * sub, sub)
                da_ref[pl.ds(at, sub), :] = d_refs[b][...]
            low = lanes((rows, 128)) < 64
            do = nt_dot(da_ref[...], wo_ref[...]).astype(BF).astype(F32)
            first = jnp.where(low, 0.0, pltpu.roll(do, 64, 1))
            second = jnp.where(low, 0.0, do)
            do_ref[:rows, :] = first.astype(BF)
            do_ref[rows:, :] = second.astype(BF)
            delta_ref[:rows, :] = jnp.broadcast_to(
                jnp.sum(first * oa_ref[:rows, :], axis=1, keepdims=True), (rows, 128)
            )
            delta_ref[rows:, :] = jnp.broadcast_to(
                jnp.sum(second * oa_ref[rows:, :], axis=1, keepdims=True), (rows, 128)
            )
            dqs_ref[...] = jnp.zeros_like(dqs_ref)
            for k in range(n_block):
                dkv_refs[k][...] = jnp.zeros_like(dkv_refs[k])

            def block(own, kv_ref, base, out_ref):
                kv = kv_ref[pl.ds(base, rows), :]
                acc_ref[...] = jnp.zeros_like(acc_ref)

                def body(c, carry):
                    at = pl.ds(pl.multiple_of(c * chunk, chunk), chunk)
                    q, d_out = qs_ref[at, :], do_ref[at, :]
                    p = masked_exp(ids_ref, info_ref, nt_dot(q, kv), c, own) * oa_ref[at, 0:1]
                    ds = (p * (nt_dot(d_out, kv) - delta_ref[at, 0:1])).astype(BF)
                    dqs_ref[at, :] += nn_dot(ds, kv)
                    acc_ref[...] += tn_dot(ds, q) + tn_dot(p.astype(BF), d_out)
                    return carry

                lax.fori_loop(0, 2 * rows // chunk, body, 0)
                out_ref[pl.ds(base, rows), :] = acc_ref[...].astype(BF)

            if blocks_mode:
                for k in range(n_block):
                    pl.when(owner(ids_ref, k) <= ids_ref[0])(
                        lambda k=k: block(owner(ids_ref, k), kv_refs[k], 0, dkv_refs[k])
                    )
            else:

                def step(j, carry):
                    block(j, kv_refs[0], pl.multiple_of(j * rows, rows), dkv_refs[0])
                    return carry

                lax.fori_loop(0, ids_ref[0] + 1, step, 0)
            dq_ref[...] = jnp.where(low, dqs_ref[:rows, :], pltpu.roll(dqs_ref[rows:, :], 64, 1))

        d_query, d_attn_full, *d_kv = call(
            attend_back,
            [((rows, 128), F32), ((rows, width), BF)]
            + [((rows * (1 if blocks_mode else n_shard), 128), BF)] * n_block,
            ids,
            [row_info, queries, out_and_inverse, own_rows, *row_blocks, *kv_parts],
            scratch=[
                pltpu.VMEM((2 * rows, 128), BF),
                pltpu.VMEM((2 * rows, 128), F32),
                pltpu.VMEM((2 * rows, 128), F32),
                pltpu.VMEM((rows, 128), F32),
            ],
            flops=10 * 2 * rows * rows * n_shard * 128,
            vmem=6,
            name="attend_back",
        )
        if blocks_mode:
            d_kv = after(d_kv, first_route)
            d_kv_parts = [d_kv[0], route(d_kv[1], ROUTE_A, True), route(d_kv[2], ROUTE_B, True)]
            d_kv_parts.append(swap(d_kv[3], "shard", 3))
            (second_route,) = after((second_route,), *d_kv_parts[1:])
            second_route = route(second_route, ROUTE_B, True)
        else:
            d_kv_parts = [lax.psum_scatter(d_kv[0], "shard", scatter_dimension=0, tiled=True)]

        fo_parts = plane_sum_parts(after(fo_halves, d_query))

        def finish(ids_ref, info_ref, mid_ref, *refs):
            part_refs, out_ref = refs[:n_tensor], refs[n_tensor]
            total = mid_ref[...] + tree([p[...] for p in part_refs])
            out_ref[...] = (info_ref[my_rows(ids_ref), 1:2] * total).astype(BF)

        (output_block,) = call(
            finish, [((sub, width), BF)], ids, [row_info, middle, *fo_parts], vmem=4, name="finish"
        )
        output_parts = plane_blocks(output_block)

        def stack_rows(ids_ref, *refs):
            for b in range(n_plane):
                at = pl.multiple_of(plane_index(ids_ref, b) * sub, sub)
                refs[-1][pl.ds(at, sub), :] = refs[b][...].astype(refs[-1].dtype)

        (block_output,) = call(
            stack_rows, [((rows, width), BF)], ids, output_parts, vmem=2, name="stack_output"
        )

        def out_grads(ids_ref, att_ref, da_ref, *outs):
            for k in range(n_block):
                outs[k][...] = tn_dot(att_ref[...], da_ref[:, pl.ds(offset(ids_ref, k), wide)]).astype(BF)

        grad_out = call(
            out_grads,
            [((q_cols, wide), BF)] * n_block,
            ids,
            [attended, d_attn_full],
            flops=2 * rows * width * q_cols,
            vmem=4,
            name="out_grads",
        )

        def project_back(ids_ref, x_ref, n_ref, raw_ref, dq_ref, cos_ref, sin_ref, hg_ref, gp_ref, *refs):
            dkv_refs, refs = refs[:n_block], refs[n_block:]
            w_refs, refs = refs[:n_block], refs[n_block:]
            if blocks_mode:
                gwo_refs, refs = refs[:n_block], refs[n_block:]
            send_ref, keep_ref, g_refs = refs[0], refs[1], refs[2 : 2 + n_block]
            low_ref, r_ref = refs[-2:]
            lane = lanes((rows, 128))
            low, first = lane < 64, (lane % 64) < 32
            cos, sin = cos_ref[...], sin_ref[...]

            def back(v, g, d):
                d = d * cos + turn_back(d * sin, first)
                r = lax.rsqrt(head_mean(v * v, low) + EPSILON)
                w = v * r
                wd = d * g
                return r * (wd - w * head_mean(wd * w, low)), jnp.sum(d * w, axis=0, keepdims=True)

            scale = 1.0 / math.sqrt(head)
            dq, gain_q = back(raw_ref[:, :128], hg_ref[0:1, :], dq_ref[...] * scale)
            dkv = tree([p[...] for p in dkv_refs])
            dk, gain_k = back(raw_ref[:, 128:], hg_ref[8:9, :], dkv)
            low_ref[:, :128] = dq.astype(BF)
            low_ref[:, 128:] = jnp.where(low, dk, dkv).astype(BF)
            gain_q = gain_q + pltpu.roll(jnp.broadcast_to(gain_q, (8, 128)), 64, 1)[0:1]
            head_row = jnp.where(low[0:1], gain_q, pltpu.roll(jnp.broadcast_to(gain_k, (8, 128)), 64, 1)[0:1])
            head_row = jnp.concatenate([head_row, jnp.zeros((1, wide - 128), F32)], axis=1)
            x = x_ref[...].astype(F32)
            r_ref[...] = jnp.broadcast_to(
                lax.rsqrt(jnp.mean(x * x, axis=1, keepdims=True) + EPSILON), (rows, 128)
            )
            for k in range(n_block):
                cols = pl.ds(offset(ids_ref, k), wide)
                g_refs[k][:wide, :] = tn_dot(n_ref[:, cols], low_ref[...]).astype(BF)
                dn = nt_dot(low_ref[...], w_refs[k][:wide, :])
                low_dn = dn.astype(BF)
                for c in range(n_heads):
                    part = low_dn[c * half : (c + 1) * half]

                    @pl.when(c == ids_ref[1])
                    def _():
                        keep_ref[:, cols] = part

                    @pl.when(c != ids_ref[1])
                    def _():
                        send_ref[:, cols] = part

                w = x_ref[:, cols].astype(F32) * r_ref[:, 0:1]
                three = [jnp.sum(dn * w, axis=0, keepdims=True), gp_ref[0:1, cols], head_row]
                if blocks_mode:
                    high = [v.astype(BF).astype(F32) for v in three]
                    rest = [a - b for a, b in zip(three, high)]
                    packed_rows = high + rest + [jnp.zeros((GAIN_ROWS - 6, wide), F32)]
                    g_refs[k][wide : wide + GAIN_ROWS, :] = jnp.concatenate(packed_rows, axis=0).astype(BF)
                    g_refs[k][wide + GAIN_ROWS :, :] = gwo_refs[k][...]
                else:
                    refs[3][...] = jnp.concatenate(three + [jnp.zeros((5, wide), F32)], axis=0)

        if blocks_mode:
            grad_shapes = [((wide + GAIN_ROWS + q_cols, 256), BF)] * n_block
        else:
            grad_shapes = [((wide, 256), BF), ((8, width), F32)]
        results = call(
            project_back,
            [((half, width), BF), ((half, width), BF)] + grad_shapes,
            ids,
            [block_input, normed_one, raw, d_query, cosine, sine, head_gains, ffn_gain_part]
            + [*d_kv_parts, *attn_parts]
            + (list(grad_out) if blocks_mode else []),
            scratch=[pltpu.VMEM((rows, 256), BF), pltpu.VMEM((rows, 128), F32)],
            flops=2 * rows * width * 512,
            vmem=6,
            name="project_back",
        )
        d1_send, d1_keep, grads = results[0], results[1], results[2:]
        d1_parts = plane_sum_parts(plane_halves(d1_keep, d1_send))
        def norm_one_back(ids_ref, x_ref, dm_ref, ga_ref, *refs):
            part_refs, ig_ref = refs[:n_tensor], refs[n_tensor]
            d = tree([p[...] for p in part_refs])
            v = x_ref[my_rows(ids_ref), :].astype(F32)
            r = lax.rsqrt(jnp.mean(v * v, axis=1, keepdims=True) + EPSILON)
            w = v * r
            wd = d * ga_ref[0:1, :]
            back = r * (wd - w * jnp.mean(wd * w, axis=1, keepdims=True))
            ig_ref[...] = (dm_ref[...] + back).astype(BF)

        (input_block,) = call(
            norm_one_back,
            [((sub, width), BF)],
            ids,
            [block_input, d_middle, ga, *d1_parts],
            vmem=3,
            name="norm_one_back",
        )
        input_parts = plane_blocks(input_block)
        if blocks_mode:
            (second_route,) = after((second_route,), input_block)
            ffn_sum = tree([ffn_own, first_route, second_route], BF)

        (input_grad,) = call(
            stack_rows, [((rows, width), F32)], ids, input_parts, vmem=2, name="stack_input"
        )

        def place_ffn(ids_ref, own_ref, other_ref, gate_ref, up_ref, down_ref):
            for c in range(n_heads):

                @pl.when(ids_ref[1] == c)
                def _():
                    low_ref, high_ref = (own_ref, other_ref) if c == 0 else (other_ref, own_ref)
                    before = lanes((depth, whole)) < hid
                    blank = jnp.zeros((depth, whole - padded), F32)
                    for i, ref in enumerate((gate_ref, up_ref)):
                        at = slice(i * hid, i * hid + padded)
                        low = jnp.concatenate([low_ref[at, :].astype(F32).T, blank], axis=1)
                        high = jnp.concatenate([high_ref[at, :].astype(F32).T, blank], axis=1)
                        ref[...] = jnp.where(before, low, pltpu.roll(high, hid, 1))
                    down_ref[:hid, :] = low_ref[whole:, :].astype(F32)
                    down_ref[hid:, :] = high_ref[whole:, :].astype(F32)

        gate_grad, up_grad, down_grad = call(
            place_ffn,
            [((depth, hidden_all), F32), ((depth, hidden_all), F32), ((hidden_all, depth), F32)],
            ids,
            [ffn_sum, swap(ffn_sum, "heads", 1)],
            vmem=12,
            name="place_ffn",
        )
        def place(ids_ref, *refs):
            b_refs, (q_ref, k_ref, v_ref, o_ref, s_ref) = refs[:n_tensor], refs[n_tensor:]
            for k in range(n_tensor):
                s_ref[ids_ref[2] ^ k] = b_refs[k][...].astype(F32)
            low = lanes((depth, 128)) < 64
            for i in range(n_tensor):
                q_ref[:, i * 128 : (i + 1) * 128] = s_ref[i, :depth, :128]
                o_ref[i * q_cols : (i + 1) * q_cols, :] = s_ref[i, depth + GAIN_ROWS :, :]
            for i in range(n_tensor // 2):
                even, odd = s_ref[2 * i, :depth, 128:], s_ref[2 * i + 1, :depth, 128:]
                k_ref[:, i * 128 : (i + 1) * 128] = jnp.where(low, even, pltpu.roll(odd, 64, 1))
                v_ref[:, i * 128 : (i + 1) * 128] = jnp.where(low, pltpu.roll(even, 64, 1), odd)

        if blocks_mode:
            grads = after(grads, d1_parts[0])
            bundle = after((shard_sum(grads),), block_output)[0]
            bundles = [bundle] + [swap(bundle, "tensor", k) for k in range(1, n_tensor)]
            bundles = [after((bundle,), input_grad, gate_grad)[0]] + bundles[1:]
            total = tree([b[depth : depth + GAIN_ROWS] for b in bundles])
            total = total + swap(total, "heads", 1)
            total = total[0:3] + total[3:6]
            attn_gain_grad, ffn_gain_grad, head_gain_grad = total[0], total[1], total[2]
            query_grad, key_grad, value_grad, out_weight_grad = call(
                place,
                [
                    ((depth, n_tensor * q_cols), F32),
                    ((depth, n_tensor * k_cols), F32),
                    ((depth, n_tensor * k_cols), F32),
                    ((n_tensor * q_cols, depth), F32),
                ],
                ids,
                bundles,
                scratch=[pltpu.VMEM((n_tensor,) + bundle.shape, F32)],
                vmem=4,
                name="place",
            )
        else:
            own_sum = lax.psum_scatter(grads[0], "shard", scatter_dimension=0, tiled=True)
            total = lax.psum(grads[1], ("shard", "heads", "tensor"))
            attn_gain_grad = lax.dynamic_slice_in_dim(total[0], z * depth, depth)
            ffn_gain_grad = lax.dynamic_slice_in_dim(total[1], z * depth, depth)
            head_gain_grad = total[2]
            found = lax.all_gather(own_sum, "tensor", axis=0).astype(F32)
            flat = lambda x: jnp.swapaxes(x, 0, 1).reshape(depth, -1)
            query_grad = flat(found[:, :, :128])
            key_grad, value_grad = flat(found[:, :, 128:192]), flat(found[:, :, 192:])
            out_sum = lax.psum_scatter(grad_out[0], "shard", scatter_dimension=1, tiled=True)
            out_weight_grad = lax.all_gather(out_sum, "tensor", axis=0, tiled=True).astype(F32)

        return (
            block_output,
            input_grad,
            attn_gain_grad,
            query_grad,
            key_grad,
            value_grad,
            head_gain_grad[:head],
            head_gain_grad[head : 2 * head],
            out_weight_grad,
            ffn_gain_grad,
            gate_grad,
            up_grad,
            down_grad,
        )

    return on_device


def solution(mesh):
    placed = (
        P("shard", None),
        P("shard"),
        P("shard", "heads"),
        P("shard", "heads"),
        P("shard", "heads"),
        P(),
        P(),
        P("heads", "shard"),
        P("shard"),
        P("shard", "tensor"),
        P("shard", "tensor"),
        P("tensor", "shard"),
        P(),
        P(),
        P("shard", None),
    )
    return jax.shard_map(
        make(mesh),
        mesh=mesh,
        in_specs=placed,
        out_specs=(
            P("shard", None),
            P("shard", None),
            P("shard"),
            P("shard", "heads"),
            P("shard", "heads"),
            P("shard", "heads"),
            P(),
            P(),
            P("heads", "shard"),
            P("shard"),
            P("shard", "tensor"),
            P("shard", "tensor"),
            P("tensor", "shard"),
        ),
        check_vma=False,
    )
```

```python
import math

import jax
import jax.numpy as jnp
import numpy as np
from jax import lax
from jax.experimental import pallas as pl
from jax.experimental.pallas import tpu as pltpu
from jax.sharding import PartitionSpec as P

EPSILON = 1e-05
ROPE_THETA = 1000000.0
BF = jnp.bfloat16
F32 = jnp.float32
MIB = 1 << 20
GAIN_ROWS = 16
ROUTE_A = [(0, 1), (1, 3), (2, 0), (3, 2)]
ROUTE_B = [(0, 2), (1, 0), (2, 3), (3, 1)]


def nn_dot(a, b):
    return lax.dot_general(a, b, (((1,), (0,)), ((), ())), preferred_element_type=F32)


def nt_dot(a, b):
    return lax.dot_general(a, b, (((1,), (1,)), ((), ())), preferred_element_type=F32)


def tn_dot(a, b):
    return lax.dot_general(a, b, (((0,), (0,)), ((), ())), preferred_element_type=F32)


def call(kernel, outs, ids, arrays, scratch=(), vmem=32, flops=0, name=None, n_hbm=0):
    shapes = [jax.ShapeDtypeStruct(s, d) for s, d in outs]
    moved = sum(a.size * a.dtype.itemsize for a in arrays)
    moved += sum(math.prod(s.shape) * s.dtype.itemsize for s in shapes)
    return pl.pallas_call(
        kernel,
        out_shape=shapes,
        in_specs=[pl.BlockSpec(memory_space=pltpu.SMEM)]
        + [pl.BlockSpec(memory_space=pltpu.HBM) for _ in range(n_hbm)]
        + [pl.BlockSpec(memory_space=pltpu.VMEM) for _ in arrays[n_hbm:]],
        out_specs=[pl.BlockSpec(memory_space=pltpu.VMEM) for _ in shapes],
        scratch_shapes=list(scratch),
        compiler_params=pltpu.CompilerParams(vmem_limit_bytes=vmem * MIB),
        cost_estimate=pl.CostEstimate(flops=int(flops), bytes_accessed=int(moved), transcendentals=0),
        name=name,
    )(ids, *arrays)


def lanes(shape):
    return lax.broadcasted_iota(jnp.int32, shape, 1)


def head_mean(v, low):
    first = jnp.sum(jnp.where(low, v, 0.0), axis=1, keepdims=True)
    second = jnp.sum(jnp.where(low, 0.0, v), axis=1, keepdims=True)
    return jnp.where(low, first, second) * (1.0 / 64.0)


def turn(v, first):
    return jnp.where(first, -pltpu.roll(v, 96, 1), pltpu.roll(v, 32, 1))


def turn_back(v, first):
    return jnp.where(first, pltpu.roll(v, 96, 1), -pltpu.roll(v, 32, 1))


def tree(values, dtype=F32):
    values = [v.astype(F32) for v in values]
    while len(values) > 1:
        pairs = [values[i] + values[i + 1] for i in range(0, len(values) - 1, 2)]
        values = pairs + values[len(values) - len(values) % 2 :]
    return values[0].astype(dtype)


def make(mesh):
    n_shard, n_heads, n_tensor = (mesh.shape[a] for a in ("shard", "heads", "tensor"))
    blocks_mode = n_shard == 4
    n_plane = n_heads * n_tensor

    def swap(x, axis, k):
        size = mesh.shape[axis]
        return lax.ppermute(x, axis, [(i, i ^ k) for i in range(size)])

    def route(x, pairs, back):
        return lax.ppermute(x, "shard", [(b, a) for a, b in pairs] if back else pairs)

    def inner():
        z = lax.axis_index("shard")
        return (z == 1) | (z == 2)

    def shard_blocks(x):
        return [x, route(x, ROUTE_A, False), route(x, ROUTE_B, False), swap(x, "shard", 3)]

    def after(values, *first):
        return lax.optimization_barrier((*values, *first))[: len(values)]

    def shard_sum(even, odd, size):
        found = swap(odd, "shard", 1)
        pairs = tree([even, found], BF)
        return tree([pairs[:size], swap(pairs[size:], "shard", 2)], BF)

    def shard_sum_staged(blocks, later):
        (found,) = after((swap(blocks[3], "shard", 1),), later)
        found = found.astype(F32)
        a = (blocks[1].astype(F32) + jnp.where(inner(), 0.0, found)).astype(BF)
        b = (blocks[2].astype(F32) + jnp.where(inner(), found, 0.0)).astype(BF)
        return blocks[0], route(a, ROUTE_A, True), b

    def plane_blocks(x):
        same = [x] + [swap(x, "tensor", k) for k in range(1, n_tensor)]
        found = list(same)
        for i in range(1, n_heads):
            found += [swap(s, "heads", i) for s in same]
        return found

    def plane_index(ids, b):
        return (ids[1] ^ (b // n_tensor)) * n_tensor + (ids[2] ^ (b % n_tensor))

    def on_device(
        block_input,
        attn_gain,
        query_weight,
        key_weight,
        value_weight,
        query_gain,
        key_gain,
        output_weight,
        ffn_gain,
        gate_weight,
        up_weight,
        down_weight,
        lengths,
        packing,
        out_grad,
    ):
        rows, width = block_input.shape
        depth = query_weight.shape[0]
        head = query_gain.shape[0]
        hidden_all = gate_weight.shape[1]
        hid = hidden_all // n_heads
        q_cols = query_weight.shape[1] // n_tensor
        k_cols = key_weight.shape[1] // n_tensor
        n_block = n_shard if blocks_mode else 1
        wide = width // n_block
        padded = -(-hid // 128) * 128
        whole = 2 * hid
        sub = rows // n_plane
        half = rows // n_heads
        step = half
        z, h, t = (lax.axis_index(a) for a in ("shard", "heads", "tensor"))
        if blocks_mode:
            ids = jnp.stack([z, h, t, z, z ^ jnp.where(inner(), 1, 2), z ^ jnp.where(inner(), 2, 1), z ^ 3])
        else:
            ids = jnp.stack([z, h, t])
        ids = ids.astype(jnp.int32)

        def owner(ids_ref, k):
            return ids_ref[3 + k]

        def offset(ids_ref, k):
            return pl.multiple_of(owner(ids_ref, k) * wide, wide) if blocks_mode else 0

        def fetch(pairs, sems):
            copies = [pltpu.make_async_copy(a, b, sems.at[i]) for i, (a, b) in enumerate(pairs)]
            for copy in copies:
                copy.start()
            return copies

        def share_attn(ids_ref, q_hbm, k_hbm, v_hbm, o_hbm, ag_hbm, fg_hbm, *outs):
            own_ref = outs[0]
            q_ref, k_ref, v_ref, ag_ref, fg_ref, sems = outs[-6:]
            i = ids_ref[2]
            tile = pl.ds(pl.multiple_of((i // 2) * 128, 128), 128)
            at = pl.multiple_of(i * q_cols, q_cols)
            out_ref = own_ref.at[depth + GAIN_ROWS :, :] if blocks_mode else outs[2]
            copies = fetch(
                [
                    (ag_hbm, ag_ref),
                    (fg_hbm, fg_ref),
                    (q_hbm.at[:, pl.ds(at, q_cols)], q_ref),
                    (k_hbm.at[:, tile], k_ref),
                    (v_hbm.at[:, tile], v_ref),
                    (o_hbm.at[pl.ds(at, q_cols), :], out_ref),
                ],
                sems,
            )
            for copy in copies:
                copy.wait()
            both = [ag_ref[...].astype(F32).reshape(1, depth), fg_ref[...].astype(F32).reshape(1, depth)]
            both = jnp.concatenate(both + [jnp.zeros((GAIN_ROWS - 2, depth), F32)], axis=0).astype(BF)
            if blocks_mode:
                own_ref[depth : depth + GAIN_ROWS, :] = both
            else:
                outs[1][...] = both
            own_ref[:depth, :128] = q_ref[...]
            k_, v_ = k_ref[...].astype(F32), v_ref[...].astype(F32)
            even = (i % 2) == 0
            low = lanes((depth, 128)) < 64
            k_ = jnp.where(even, k_, pltpu.roll(k_, 64, 1))
            v_ = jnp.where(even, pltpu.roll(v_, 64, 1), v_)
            own_ref[:depth, 128:] = jnp.where(low, k_, v_).astype(BF)

        if blocks_mode:
            share_shapes = [((depth + GAIN_ROWS + q_cols, 256), BF)]
        else:
            share_shapes = [((depth, 256), BF), ((GAIN_ROWS, depth), BF), ((q_cols, depth), BF)]
        own_attn, *own_more = call(
            share_attn,
            share_shapes,
            ids,
            [query_weight, key_weight, value_weight, output_weight, attn_gain, ffn_gain],
            scratch=[pltpu.VMEM((depth, 128), BF)] * 3
            + [pltpu.VMEM((depth,), BF)] * 2
            + [pltpu.SemaphoreType.DMA((6,))],
            vmem=56,
            n_hbm=6,
            name="share_attn",
        )

        def share_ffn(ids_ref, g_hbm, u_hbm, d_hbm, own_ref, g_ref, u_ref, sems):
            rows_ = pl.ds(pl.multiple_of(ids_ref[1] * hid, 16), hid)
            pairs = [(g_hbm, g_ref), (u_hbm, u_ref), (d_hbm.at[rows_, :], own_ref.at[whole:, :])]
            for copy in fetch(pairs, sems):
                copy.wait()
            for i, ref in enumerate((g_ref, u_ref)):
                part = ref[...].astype(F32)
                part = jnp.where(ids_ref[1] == 0, part, pltpu.roll(part, hid, 1))[:, :padded]
                own_ref[i * hid : (i + 1) * hid, :] = part.T[:hid].astype(BF)

        (own_ffn,) = call(
            share_ffn,
            [((whole + hid, depth), BF)],
            ids,
            [gate_weight, up_weight, down_weight],
            scratch=[
                pltpu.VMEM((depth, whole), BF),
                pltpu.VMEM((depth, whole), BF),
                pltpu.SemaphoreType.DMA((3,)),
            ],
            vmem=8,
            n_hbm=3,
            name="share_ffn",
        )

        count = lengths.shape[0]
        frequency = np.power(np.float64(ROPE_THETA), -np.arange(head // 2) * (2.0 / head))
        frequency = jnp.asarray(np.tile(frequency, 4)[None].astype(np.float32))

        def layout(ids_ref, len_hbm, pack_hbm, freq_hbm, qg_hbm, kg_hbm, *refs):
            info_ref, angle_ref, hg_ref, len_ref, pack_ref, freq_ref, qg_ref, kg_ref, sems = refs
            pairs = [(len_hbm, len_ref), (pack_hbm, pack_ref), (freq_hbm, freq_ref), (qg_hbm, qg_ref), (kg_hbm, kg_ref)]
            for copy in fetch(pairs, sems):
                copy.wait()
            token = ids_ref[0] * rows + lax.broadcasted_iota(jnp.int32, (rows, 128), 0)
            start = jnp.zeros((rows, 128), jnp.int32)
            end = jnp.int32(0)
            for j in range(count):
                end = end + len_ref[pack_ref[j]]
                start = jnp.where(token >= end, end, start)
            live = token < end
            lowest = jnp.where(live, start, token).astype(F32)
            info_ref[...] = jnp.where(lanes((rows, 128)) == 0, lowest, live.astype(F32))
            angle_ref[...] = (token - start).astype(F32) * freq_ref[...]
            q, k_ = qg_ref[...].astype(F32).reshape(1, head), kg_ref[...].astype(F32).reshape(1, head)
            q = jnp.concatenate([q, q], axis=1)
            k_ = jnp.concatenate([k_, jnp.ones((1, head), F32)], axis=1)
            hg_ref[:8, :] = jnp.broadcast_to(q, (8, 128))
            hg_ref[8:, :] = jnp.broadcast_to(k_, (8, 128))

        row_info, angles, head_gains = call(
            layout,
            [((rows, 128), F32), ((rows, 128), F32), ((16, 128), F32)],
            ids,
            [lengths, packing, frequency, query_gain, key_gain],
            scratch=[
                pltpu.SMEM((count,), jnp.int32),
                pltpu.SMEM((count,), jnp.int32),
                pltpu.VMEM((1, 128), F32),
                pltpu.VMEM((head,), BF),
                pltpu.VMEM((head,), BF),
                pltpu.SemaphoreType.DMA((5,)),
            ],
            vmem=2,
            n_hbm=5,
            name="layout",
        )
        cosine, sine = jnp.cos(angles), jnp.sin(angles)

        if blocks_mode:
            attn_parts = shard_blocks(own_attn)
            gain_parts = []
        else:
            gather = lambda x, axis: [lax.all_gather(x, "shard", axis=axis, tiled=True)]
            attn_parts = gather(own_attn, 0)
            gain_parts = gather(own_more[0], 1)
            out_parts = gather(own_more[1], 1)
            ffn_parts = gather(own_ffn, 1)

        def project(ids_ref, x_ref, cos_ref, sin_ref, hg_ref, *refs):
            w_refs, refs = refs[:n_block], refs[n_block:]
            g_refs, refs = refs[: len(gain_parts)], refs[len(gain_parts) :]
            n_ref, raw_ref, qs_ref, kv_ref, ga_ref, gf_ref = refs
            for k in range(n_block):
                both = (g_refs[0][...] if g_refs else w_refs[k][wide : wide + GAIN_ROWS, :]).astype(F32)
                where = pl.ds(offset(ids_ref, k), wide)
                ga_ref[:, where] = jnp.broadcast_to(both[0:1], (8, wide))
                gf_ref[:, where] = jnp.broadcast_to(both[1:2], (8, wide))
            step = 128

            def body(c, carry):
                at = pl.ds(pl.multiple_of(c * step, step), step)
                x = x_ref[at, :].astype(F32)
                r = lax.rsqrt(jnp.mean(x * x, axis=1, keepdims=True) + EPSILON)
                n_ref[at, :] = (x * r * ga_ref[0:1, :]).astype(BF)
                acc = jnp.zeros((step, 256), F32)
                for k in range(n_block):
                    acc += nn_dot(n_ref[at, pl.ds(offset(ids_ref, k), wide)], w_refs[k][:wide, :])
                raw_ref[at, :] = acc
                lane = lanes((step, 128))
                low, first = lane < 64, (lane % 64) < 32
                cos, sin = cos_ref[at, :], sin_ref[at, :]
                q, kv = acc[:, :128], acc[:, 128:]
                q = q * lax.rsqrt(head_mean(q * q, low) + EPSILON) * hg_ref[0:1, :]
                q = (q * cos + turn(q, first) * sin).astype(BF).astype(F32) * (1.0 / math.sqrt(head))
                qs_ref[at, :] = jnp.where(low, q, 0.0).astype(BF)
                qs_ref[pl.ds(pl.multiple_of(rows + c * step, step), step), :] = jnp.where(
                    low, pltpu.roll(q, 64, 1), 0.0
                ).astype(BF)
                k_ = kv * lax.rsqrt(head_mean(kv * kv, low) + EPSILON) * hg_ref[8:9, :]
                k_ = k_ * cos + turn(k_, first) * sin
                kv_ref[at, :] = jnp.where(low, k_, kv).astype(BF)
                return carry

            lax.fori_loop(0, rows // step, body, 0)

        normed_one, raw, queries, own_kv, ga, gf = call(
            project,
            [
                ((rows, width), BF),
                ((rows, 256), F32),
                ((2 * rows, 128), BF),
                ((rows, 128), BF),
                ((8, width), F32),
                ((8, width), F32),
            ],
            ids,
            [block_input, cosine, sine, head_gains, *attn_parts, *gain_parts],
            flops=2 * rows * width * 256,
            vmem=4,
            name="project",
        )
        if blocks_mode:
            kv_parts = shard_blocks(own_kv)
            (own_ffn,) = after((own_ffn,), own_kv)
            ffn_a, ffn_b = route(own_ffn, ROUTE_A, False), route(own_ffn, ROUTE_B, False)
        else:
            kv_parts = [lax.all_gather(own_kv, "shard", axis=0, tiled=True)]

        if blocks_mode:

            def beside(ids_ref, *refs):
                for k in range(n_block):
                    refs[-1][:, pl.ds(offset(ids_ref, k), wide)] = refs[k][wide + GAIN_ROWS :, :]

            late = after(attn_parts, *kv_parts[1:])
            (own_rows,) = call(beside, [((q_cols, width), BF)], ids, late, vmem=1, name="beside")
        else:
            own_rows = out_parts[0]
        row_parts = [own_rows] + [swap(own_rows, "tensor", k) for k in range(1, n_tensor)]

        def below(ids_ref, *refs):
            for k in range(n_tensor):
                at = pl.multiple_of((ids_ref[2] ^ k) * q_cols, q_cols)
                refs[-1][pl.ds(at, q_cols), :] = refs[k][...]

        (out_half,) = call(
            below, [((n_tensor * q_cols, width), BF)], ids, row_parts, vmem=1, name="below"
        )
        out_halves = [out_half, swap(out_half, "heads", 1)]

        chunk = 256

        def over_keys(ids_ref, kv_refs, block):
            if blocks_mode:
                for k in range(n_block):
                    pl.when(owner(ids_ref, k) <= ids_ref[0])(
                        lambda k=k: block(owner(ids_ref, k), kv_refs[k], 0)
                    )
            else:

                def step(j, carry):
                    block(j, kv_refs[0], pl.multiple_of(j * rows, rows))
                    return carry

                lax.fori_loop(0, ids_ref[0] + 1, step, 0)

        def masked_exp(ids_ref, info_ref, score, c, own):
            row = (c * chunk) % rows
            at = pl.ds(pl.multiple_of(row, chunk), chunk)
            col = lanes((chunk, rows))
            lowest_ = info_ref[at, 0:1].astype(jnp.int32) - own * rows
            mine = lax.broadcasted_iota(jnp.int32, (chunk, 1), 0) + (row + (ids_ref[0] - own) * rows)
            return jnp.where((col >= lowest_) & (col <= mine), jnp.exp(score), 0.0)

        def attend(ids_ref, info_ref, qs_ref, *refs):
            kv_refs, (att_ref, oa_ref, acc_ref) = refs[:n_block], refs[n_block:]
            acc_ref[...] = jnp.zeros_like(acc_ref)
            low = lanes((rows, 128)) < 64

            def block(own, kv_ref, base):
                kv = kv_ref[pl.ds(base, rows), :]
                counted = jnp.where(low, 1.0, kv.astype(F32)).astype(BF)

                def body(c, carry):
                    at = pl.ds(pl.multiple_of(c * chunk, chunk), chunk)
                    p = masked_exp(ids_ref, info_ref, nt_dot(qs_ref[at, :], kv), c, own)
                    acc_ref[at, :] += nn_dot(p.astype(BF), counted)
                    return carry

                lax.fori_loop(0, 2 * rows // chunk, body, 0)

            over_keys(ids_ref, kv_refs, block)
            for i in range(2):
                acc = acc_ref[i * rows : (i + 1) * rows, :]
                inverse = 1.0 / jnp.where(low, acc, 1.0)
                done = jnp.where(low, inverse, acc * pltpu.roll(inverse, 64, 1))
                oa_ref[i * rows : (i + 1) * rows, :] = done
            att_ref[...] = jnp.where(
                low, pltpu.roll(oa_ref[:rows, :], 64, 1), oa_ref[rows:, :]
            ).astype(BF)

        attended, out_and_inverse = call(
            attend,
            [((rows, 128), BF), ((2 * rows, 128), F32)],
            ids,
            [row_info, queries, *kv_parts],
            scratch=[pltpu.VMEM((2 * rows, 128), F32)],
            flops=120 * 2 * rows * rows * n_shard * 128,
            vmem=4,
            name="attend",
        )
        attended_parts = plane_blocks(attended)

        def my_rows(ids_ref):
            return pl.ds(pl.multiple_of((ids_ref[1] * n_tensor + ids_ref[2]) * sub, sub), sub)

        def middle_part(ids_ref, x_ref, gf_ref, *refs):
            wo_refs, refs = refs[:n_heads], refs[n_heads:]
            a_refs, (n2_ref, mid_ref, a_ref, m_ref) = refs[:n_plane], refs[n_plane:]
            deep = n_tensor * q_cols
            for b in range(n_plane):
                at = pl.multiple_of(plane_index(ids_ref, b) * q_cols, q_cols)
                a_ref[:, pl.ds(at, q_cols)] = a_refs[b][...]

            def body(c, carry):
                at = pl.ds(pl.multiple_of(c * step, step), step)
                parts = [
                    nn_dot(a_ref[at, pl.ds(pl.multiple_of((ids_ref[1] ^ i) * deep, deep), deep)], wo_refs[i][...])
                    for i in range(n_heads)
                ]
                middle = x_ref[at, :].astype(F32) + tree(parts)
                m_ref[at, :] = middle
                r = lax.rsqrt(jnp.mean(middle * middle, axis=1, keepdims=True) + EPSILON)
                n2_ref[at, :] = (middle * r * gf_ref[0:1, :]).astype(BF)
                return carry

            lax.fori_loop(0, n_heads, body, 0)
            mid_ref[...] = m_ref[my_rows(ids_ref), :]

        normed_two, middle = call(
            middle_part,
            [((rows, width), BF), ((sub, width), F32)],
            ids,
            [block_input, gf, *out_halves, *attended_parts],
            scratch=[pltpu.VMEM((rows, width), BF), pltpu.VMEM((rows, width), F32)],
            flops=2 * rows * width * width,
            vmem=8,
            name="middle",
        )

        if blocks_mode:
            (chosen,) = after((jnp.where(inner(), ffn_b, ffn_a),), *attended_parts[1:n_tensor])
            ffn_parts = [own_ffn, ffn_a, ffn_b, swap(chosen, "shard", 1)]

        def feed_forward(ids_ref, info_ref, og_ref, n2_ref, *refs):
            w_refs, refs = refs[:n_block], refs[n_block:]
            send_ref, keep_ref, dg_ref, du_ref, hid_ref, cot_ref, both_ref = refs

            def body(c, carry):
                at = pl.ds(pl.multiple_of(c * step, step), step)
                cot_ref[at, :] = (og_ref[at, :].astype(F32) * info_ref[at, 1:2]).astype(BF)
                gate = up = dh = jnp.zeros((step, hid), F32)
                for k in range(n_block):
                    cols = pl.ds(offset(ids_ref, k), wide)
                    gate += nt_dot(n2_ref[at, cols], w_refs[k][:hid, :])
                    up += nt_dot(n2_ref[at, cols], w_refs[k][hid:whole, :])
                    dh += nt_dot(cot_ref[at, cols], w_refs[k][whole:, :])
                sig = 1.0 / (1.0 + jnp.exp(-gate))
                act = gate * sig
                hid_ref[at, :] = (act * up).astype(BF)
                dg_ref[at, :] = (dh * up * sig * (1.0 + gate * (1.0 - sig))).astype(BF)
                du_ref[at, :] = (dh * act).astype(BF)
                for k in range(n_block):
                    off = offset(ids_ref, k)
                    dn = nn_dot(dg_ref[at, :], w_refs[k][:hid, :]) + nn_dot(du_ref[at, :], w_refs[k][hid:whole, :])
                    both_ref[:, pl.ds(off, wide)] = dn.astype(BF)
                    off = pl.multiple_of(width + off, wide)
                    both_ref[:, pl.ds(off, wide)] = nn_dot(hid_ref[at, :], w_refs[k][whole:, :]).astype(BF)

                @pl.when(c == ids_ref[1])
                def _():
                    keep_ref[...] = both_ref[...]

                @pl.when(c != ids_ref[1])
                def _():
                    send_ref[...] = both_ref[...]

                return carry

            lax.fori_loop(0, n_heads, body, 0)

        both_send, both_keep, d_gate, d_up, hidden, cot = call(
            feed_forward,
            [
                ((half, 2 * width), BF),
                ((half, 2 * width), BF),
                ((rows, hid), BF),
                ((rows, hid), BF),
                ((rows, hid), BF),
                ((rows, width), BF),
            ],
            ids,
            [row_info, out_grad, normed_two, *ffn_parts],
            scratch=[pltpu.VMEM((half, 2 * width), BF)],
            flops=2 * rows * width * 6 * hid,
            vmem=14,
            name="feed_forward",
        )

        def split(ids_ref, keep_ref, got_ref, *outs):
            for k in range(n_tensor):
                at = pl.ds(pl.multiple_of((ids_ref[2] ^ k) * sub, sub), sub)
                total = keep_ref[at, :].astype(F32) + got_ref[at, :].astype(F32)
                outs[k][...] = total.astype(BF)

        def plane_halves(keep, send):
            got = swap(send, "heads", 1)
            shape = (sub, keep.shape[1])
            return call(split, [(shape, BF)] * n_tensor, ids, [keep, got], vmem=4, name="split")

        def plane_sum_parts(parts):
            return [parts[0]] + [swap(parts[k], "tensor", k) for k in range(1, n_tensor)]

        both_parts = plane_sum_parts(plane_halves(both_keep, both_send))

        def ffn_grads(ids_ref, n2_ref, cot_ref, dg_ref, du_ref, hid_ref, *outs):
            outs, turned_ref = outs[:-1], outs[-1]
            for i, ref in enumerate((dg_ref, du_ref, hid_ref)):
                turned_ref[i * hid : (i + 1) * hid, :] = ref[...].T
            for k in range(n_block):
                cols = pl.ds(offset(ids_ref, k), wide)
                outs[k][:whole, :] = nn_dot(turned_ref[:whole, :], n2_ref[:, cols]).astype(BF)
                outs[k][whole:, :] = nn_dot(turned_ref[whole:, :], cot_ref[:, cols]).astype(BF)

        grad_ffn = call(
            ffn_grads,
            [((whole + hid, wide), BF)] * n_block,
            ids,
            [normed_two, cot, d_gate, d_up, hidden],
            scratch=[pltpu.VMEM((whole + hid, rows), BF)],
            flops=2 * rows * width * 3 * hid,
            vmem=8,
            name="ffn_grads",
        )
        (first_part,) = after((both_parts[0],), grad_ffn[0])
        both_parts = [first_part] + both_parts[1:]

        def norm_two_back(ids_ref, info_ref, mid_ref, cot_ref, gf_ref, *refs):
            part_refs, (dm_ref, da_ref, gp_ref, bo_ref) = refs[:n_tensor], refs[n_tensor:]
            d = tree([p[:, :width] for p in part_refs])
            v = mid_ref[...]
            r = lax.rsqrt(jnp.mean(v * v, axis=1, keepdims=True) + EPSILON)
            w = v * r
            wd = d * gf_ref[0:1, :]
            cot_ = cot_ref[my_rows(ids_ref), :].astype(F32)
            dm = cot_ + r * (wd - w * jnp.mean(wd * w, axis=1, keepdims=True))
            dm_ref[...] = dm
            da_ref[...] = dm.astype(BF)
            gp_ref[...] = jnp.broadcast_to(jnp.sum(d * w, axis=0, keepdims=True), gp_ref.shape)
            total = v + tree([p[:, width:] for p in part_refs])
            bo_ref[...] = (info_ref[my_rows(ids_ref), 1:2] * total).astype(BF)

        d_middle, d_attn, ffn_gain_part, output_block = call(
            norm_two_back,
            [((sub, width), F32), ((sub, width), BF), ((8, width), F32), ((sub, width), BF)],
            ids,
            [row_info, middle, cot, gf, *both_parts],
            vmem=4,
            name="norm_two_back",
        )
        if blocks_mode:
            ffn_own, first_route, second_route = shard_sum_staged(grad_ffn, d_attn)
        else:
            ffn_sum = lax.psum_scatter(grad_ffn[0], "shard", scatter_dimension=1, tiled=True)
        row_blocks = plane_blocks(d_attn)

        def attend_back(ids_ref, info_ref, qs_ref, oa_ref, wo_ref, *refs):
            d_refs, refs = refs[:n_plane], refs[n_plane:]
            kv_refs, refs = refs[:n_block], refs[n_block:]
            dq_ref, da_ref, dkv_refs = refs[0], refs[1], refs[2 : 2 + n_block]
            do_ref, delta_ref, dqs_ref, acc_ref = refs[2 + n_block :]
            for b in range(n_plane):
                at = pl.multiple_of(plane_index(ids_ref, b) * sub, sub)
                da_ref[pl.ds(at, sub), :] = d_refs[b][...]
            low = lanes((rows, 128)) < 64
            do = nt_dot(da_ref[...], wo_ref[...]).astype(BF).astype(F32)
            first = jnp.where(low, 0.0, pltpu.roll(do, 64, 1))
            second = jnp.where(low, 0.0, do)
            do_ref[:rows, :] = first.astype(BF)
            do_ref[rows:, :] = second.astype(BF)
            delta_ref[:rows, :] = jnp.broadcast_to(
                jnp.sum(first * oa_ref[:rows, :], axis=1, keepdims=True), (rows, 128)
            )
            delta_ref[rows:, :] = jnp.broadcast_to(
                jnp.sum(second * oa_ref[rows:, :], axis=1, keepdims=True), (rows, 128)
            )
            dqs_ref[...] = jnp.zeros_like(dqs_ref)
            for k in range(n_block):
                dkv_refs[k][...] = jnp.zeros_like(dkv_refs[k])

            def block(own, kv_ref, base, out_ref):
                kv = kv_ref[pl.ds(base, rows), :]
                acc_ref[...] = jnp.zeros_like(acc_ref)

                def body(c, carry):
                    at = pl.ds(pl.multiple_of(c * chunk, chunk), chunk)
                    q, d_out = qs_ref[at, :], do_ref[at, :]
                    p = masked_exp(ids_ref, info_ref, nt_dot(q, kv), c, own) * oa_ref[at, 0:1]
                    ds = (p * (nt_dot(d_out, kv) - delta_ref[at, 0:1])).astype(BF)
                    dqs_ref[at, :] += nn_dot(ds, kv)
                    acc_ref[...] += tn_dot(ds, q) + tn_dot(p.astype(BF), d_out)
                    return carry

                lax.fori_loop(0, 2 * rows // chunk, body, 0)
                out_ref[pl.ds(base, rows), :] = acc_ref[...].astype(BF)

            if blocks_mode:
                for k in range(n_block):
                    pl.when(owner(ids_ref, k) <= ids_ref[0])(
                        lambda k=k: block(owner(ids_ref, k), kv_refs[k], 0, dkv_refs[k])
                    )
            else:

                def step(j, carry):
                    block(j, kv_refs[0], pl.multiple_of(j * rows, rows), dkv_refs[0])
                    return carry

                lax.fori_loop(0, ids_ref[0] + 1, step, 0)
            dq_ref[...] = jnp.where(low, dqs_ref[:rows, :], pltpu.roll(dqs_ref[rows:, :], 64, 1))

        d_query, d_attn_full, *d_kv = call(
            attend_back,
            [((rows, 128), F32), ((rows, width), BF)]
            + [((rows * (1 if blocks_mode else n_shard), 128), BF)] * n_block,
            ids,
            [row_info, queries, out_and_inverse, own_rows, *row_blocks, *kv_parts],
            scratch=[
                pltpu.VMEM((2 * rows, 128), BF),
                pltpu.VMEM((2 * rows, 128), F32),
                pltpu.VMEM((2 * rows, 128), F32),
                pltpu.VMEM((rows, 128), F32),
            ],
            flops=10 * 2 * rows * rows * n_shard * 128,
            vmem=6,
            name="attend_back",
        )
        if blocks_mode:
            d_kv = after(d_kv, first_route)
            d_kv_parts = [d_kv[0], route(d_kv[1], ROUTE_A, True), route(d_kv[2], ROUTE_B, True)]
            d_kv_parts.append(swap(d_kv[3], "shard", 3))
            (second_route,) = after((second_route,), d_query)
            second_route = route(second_route, ROUTE_B, True)
        else:
            d_kv_parts = [lax.psum_scatter(d_kv[0], "shard", scatter_dimension=0, tiled=True)]

        def out_grads(ids_ref, att_ref, da_ref, *outs):
            for k in range(n_block):
                outs[k][...] = tn_dot(att_ref[...], da_ref[:, pl.ds(offset(ids_ref, k), wide)]).astype(BF)

        grad_out = call(
            out_grads,
            [((q_cols, wide), BF)] * n_block,
            ids,
            [attended, d_attn_full],
            flops=2 * rows * width * q_cols,
            vmem=4,
            name="out_grads",
        )

        bundle_rows = wide + GAIN_ROWS + q_cols

        def project_back(ids_ref, x_ref, n_ref, raw_ref, dq_ref, cos_ref, sin_ref, hg_ref, gp_ref, *refs):
            dkv_refs, refs = refs[:n_block], refs[n_block:]
            w_refs, refs = refs[:n_block], refs[n_block:]
            if blocks_mode:
                gwo_refs, refs = refs[:n_block], refs[n_block:]
            send_ref, keep_ref, g_refs = refs[0], refs[1], refs[2:-2]
            low_ref, r_ref = refs[-2:]
            lane = lanes((rows, 128))
            low, first = lane < 64, (lane % 64) < 32
            cos, sin = cos_ref[...], sin_ref[...]

            def back(v, g, d):
                d = d * cos + turn_back(d * sin, first)
                r = lax.rsqrt(head_mean(v * v, low) + EPSILON)
                w = v * r
                wd = d * g
                return r * (wd - w * head_mean(wd * w, low)), jnp.sum(d * w, axis=0, keepdims=True)

            scale = 1.0 / math.sqrt(head)
            dq, gain_q = back(raw_ref[:, :128], hg_ref[0:1, :], dq_ref[...] * scale)
            dkv = tree([p[...] for p in dkv_refs])
            dk, gain_k = back(raw_ref[:, 128:], hg_ref[8:9, :], dkv)
            low_ref[:, :128] = dq.astype(BF)
            low_ref[:, 128:] = jnp.where(low, dk, dkv).astype(BF)
            gain_q = gain_q + pltpu.roll(jnp.broadcast_to(gain_q, (8, 128)), 64, 1)[0:1]
            head_row = jnp.where(low[0:1], gain_q, pltpu.roll(jnp.broadcast_to(gain_k, (8, 128)), 64, 1)[0:1])
            head_row = jnp.concatenate([head_row, jnp.zeros((1, wide - 128), F32)], axis=1)
            x = x_ref[...].astype(F32)
            r_ref[...] = jnp.broadcast_to(
                lax.rsqrt(jnp.mean(x * x, axis=1, keepdims=True) + EPSILON), (rows, 128)
            )
            for k in range(n_block):
                cols = pl.ds(offset(ids_ref, k), wide)
                main = tn_dot(n_ref[:, cols], low_ref[...]).astype(BF)
                dn = nt_dot(low_ref[...], w_refs[k][:wide, :])
                low_dn = dn.astype(BF)
                for c in range(n_heads):
                    part = low_dn[c * half : (c + 1) * half]

                    @pl.when(c == ids_ref[1])
                    def _():
                        keep_ref[:, cols] = part

                    @pl.when(c != ids_ref[1])
                    def _():
                        send_ref[:, cols] = part

                w = x_ref[:, cols].astype(F32) * r_ref[:, 0:1]
                three = [jnp.sum(dn * w, axis=0, keepdims=True), gp_ref[0:1, cols], head_row]
                if blocks_mode:
                    high = [v.astype(BF).astype(F32) for v in three]
                    rest = [a - b for a, b in zip(three, high)]
                    packed_rows = high + rest + [jnp.zeros((GAIN_ROWS - 6, wide), F32)]
                    packed_rows = jnp.concatenate(packed_rows, axis=0).astype(BF)
                    apart = owner(ids_ref, k) ^ ids_ref[0]
                    for place_ in range(n_block):

                        @pl.when(apart == place_)
                        def _():
                            to, at = g_refs[place_ % 2], (place_ // 2) * bundle_rows
                            to[at : at + wide, :] = main
                            to[at + wide : at + wide + GAIN_ROWS, :] = packed_rows
                            to[at + wide + GAIN_ROWS : at + bundle_rows, :] = gwo_refs[k][...]

                else:
                    g_refs[0][...] = main
                    refs[3][...] = jnp.concatenate(three + [jnp.zeros((5, wide), F32)], axis=0)

        if blocks_mode:
            grad_shapes = [((2 * bundle_rows, 256), BF)] * 2
        else:
            grad_shapes = [((wide, 256), BF), ((8, width), F32)]
        results = call(
            project_back,
            [((half, width), BF), ((half, width), BF)] + grad_shapes,
            ids,
            [block_input, normed_one, raw, d_query, cosine, sine, head_gains, ffn_gain_part]
            + [*d_kv_parts, *attn_parts]
            + (list(grad_out) if blocks_mode else []),
            scratch=[pltpu.VMEM((rows, 256), BF), pltpu.VMEM((rows, 128), F32)],
            flops=60 * rows * width * 512,
            vmem=6,
            name="project_back",
        )
        d1_send, d1_keep, grads = results[0], results[1], results[2:]
        d1_parts = plane_sum_parts(plane_halves(d1_keep, d1_send))
        def norm_one_back(ids_ref, x_ref, dm_ref, ga_ref, bo_ref, *refs):
            part_refs, both_ref = refs[:n_tensor], refs[n_tensor]
            d = tree([p[...] for p in part_refs])
            v = x_ref[my_rows(ids_ref), :].astype(F32)
            r = lax.rsqrt(jnp.mean(v * v, axis=1, keepdims=True) + EPSILON)
            w = v * r
            wd = d * ga_ref[0:1, :]
            back = r * (wd - w * jnp.mean(wd * w, axis=1, keepdims=True))
            both_ref[:, :width] = (dm_ref[...] + back).astype(BF)
            both_ref[:, width:] = bo_ref[...]

        (both_block,) = call(
            norm_one_back,
            [((sub, 2 * width), BF)],
            ids,
            [block_input, d_middle, ga, output_block, *d1_parts],
            vmem=3,
            name="norm_one_back",
        )
        both_parts = plane_blocks(both_block)
        if blocks_mode:
            (second_route,) = after((second_route,), both_block)
            ffn_sum = tree([ffn_own, first_route, second_route], BF)

        def stack_rows(ids_ref, *refs):
            ig_ref, bo_ref = refs[n_plane:]
            for b in range(n_plane):
                at = pl.ds(pl.multiple_of(plane_index(ids_ref, b) * sub, sub), sub)
                ig_ref[at, :] = refs[b][:, :width].astype(F32)
                bo_ref[at, :] = refs[b][:, width:]

        input_grad, block_output = call(
            stack_rows,
            [((rows, width), F32), ((rows, width), BF)],
            ids,
            both_parts,
            vmem=8,
            name="stack_rows",
        )

        def place_ffn(ids_ref, own_ref, other_ref, gate_ref, up_ref, down_ref):
            for c in range(n_heads):

                @pl.when(ids_ref[1] == c)
                def _():
                    low_ref, high_ref = (own_ref, other_ref) if c == 0 else (other_ref, own_ref)
                    before = lanes((depth, whole)) < hid
                    blank = jnp.zeros((depth, whole - padded), F32)
                    for i, ref in enumerate((gate_ref, up_ref)):
                        at = slice(i * hid, i * hid + padded)
                        low = jnp.concatenate([low_ref[at, :].astype(F32).T, blank], axis=1)
                        high = jnp.concatenate([high_ref[at, :].astype(F32).T, blank], axis=1)
                        ref[...] = jnp.where(before, low, pltpu.roll(high, hid, 1))
                    down_ref[:hid, :] = low_ref[whole:, :].astype(F32)
                    down_ref[hid:, :] = high_ref[whole:, :].astype(F32)

        gate_grad, up_grad, down_grad = call(
            place_ffn,
            [((depth, hidden_all), F32), ((depth, hidden_all), F32), ((hidden_all, depth), F32)],
            ids,
            [ffn_sum, swap(ffn_sum, "heads", 1)],
            vmem=12,
            name="place_ffn",
        )
        def place(ids_ref, *refs):
            b_refs, (q_ref, k_ref, v_ref, o_ref, s_ref) = refs[:n_tensor], refs[n_tensor:]
            for k in range(n_tensor):
                s_ref[ids_ref[2] ^ k] = b_refs[k][...].astype(F32)
            low = lanes((depth, 128)) < 64
            for i in range(n_tensor):
                q_ref[:, i * 128 : (i + 1) * 128] = s_ref[i, :depth, :128]
                o_ref[i * q_cols : (i + 1) * q_cols, :] = s_ref[i, depth + GAIN_ROWS :, :]
            for i in range(n_tensor // 2):
                even, odd = s_ref[2 * i, :depth, 128:], s_ref[2 * i + 1, :depth, 128:]
                k_ref[:, i * 128 : (i + 1) * 128] = jnp.where(low, even, pltpu.roll(odd, 64, 1))
                v_ref[:, i * 128 : (i + 1) * 128] = jnp.where(low, pltpu.roll(even, 64, 1), odd)

        if blocks_mode:
            bundle = shard_sum(grads[0], grads[1], bundle_rows)
            bundles = [bundle] + [swap(bundle, "tensor", k) for k in range(1, n_tensor)]
            bundles = [after((bundle,), input_grad, gate_grad)[0]] + bundles[1:]
            total = tree([b[depth : depth + GAIN_ROWS] for b in bundles])
            total = total + swap(total, "heads", 1)
            total = total[0:3] + total[3:6]
            attn_gain_grad, ffn_gain_grad, head_gain_grad = total[0], total[1], total[2]
            query_grad, key_grad, value_grad, out_weight_grad = call(
                place,
                [
                    ((depth, n_tensor * q_cols), F32),
                    ((depth, n_tensor * k_cols), F32),
                    ((depth, n_tensor * k_cols), F32),
                    ((n_tensor * q_cols, depth), F32),
                ],
                ids,
                bundles,
                scratch=[pltpu.VMEM((n_tensor,) + bundle.shape, F32)],
                vmem=4,
                name="place",
            )
        else:
            own_sum = lax.psum_scatter(grads[0], "shard", scatter_dimension=0, tiled=True)
            total = lax.psum(grads[1], ("shard", "heads", "tensor"))
            attn_gain_grad = lax.dynamic_slice_in_dim(total[0], z * depth, depth)
            ffn_gain_grad = lax.dynamic_slice_in_dim(total[1], z * depth, depth)
            head_gain_grad = total[2]
            found = lax.all_gather(own_sum, "tensor", axis=0).astype(F32)
            flat = lambda x: jnp.swapaxes(x, 0, 1).reshape(depth, -1)
            query_grad = flat(found[:, :, :128])
            key_grad, value_grad = flat(found[:, :, 128:192]), flat(found[:, :, 192:])
            out_sum = lax.psum_scatter(grad_out[0], "shard", scatter_dimension=1, tiled=True)
            out_weight_grad = lax.all_gather(out_sum, "tensor", axis=0, tiled=True).astype(F32)

        return (
            block_output,
            input_grad,
            attn_gain_grad,
            query_grad,
            key_grad,
            value_grad,
            head_gain_grad[:head],
            head_gain_grad[head : 2 * head],
            out_weight_grad,
            ffn_gain_grad,
            gate_grad,
            up_grad,
            down_grad,
        )

    return on_device


def solution(mesh):
    placed = (
        P("shard", None),
        P("shard"),
        P("shard", "heads"),
        P("shard", "heads"),
        P("shard", "heads"),
        P(),
        P(),
        P("heads", "shard"),
        P("shard"),
        P("shard", "tensor"),
        P("shard", "tensor"),
        P("tensor", "shard"),
        P(),
        P(),
        P("shard", None),
    )
    return jax.shard_map(
        make(mesh),
        mesh=mesh,
        in_specs=placed,
        out_specs=(
            P("shard", None),
            P("shard", None),
            P("shard"),
            P("shard", "heads"),
            P("shard", "heads"),
            P("shard", "heads"),
            P(),
            P(),
            P("heads", "shard"),
            P("shard"),
            P("shard", "tensor"),
            P("shard", "tensor"),
            P("tensor", "shard"),
        ),
        check_vma=False,
    )
```
